256 devices in a mesh: slab: 8 (over x, y_lo), brick: 32 (over y_hi, z, core).
Axes of the slice: x: 4, y: 4 (y_hi: 2, y_lo: 2; y = y_hi * 2 + y_lo), z: 8, core: 2. Of those that a mesh axis runs over, the one named last changes fastest.
Arguments:
- positions: float32 [16384, 3, 128], P(('slab', 'brick')), may hold values from 0 to 9
- velocities: float32 [16384, 3, 128], P(('slab', 'brick')), may hold values from -6 to 6
- radius: float32 [16384, 128], P(('slab', 'brick')), may hold values from 0.35 to 0.65
- owners: int32 [16384], P(('slab', 'brick')), may hold values from 0 to 31, as said below
- neighbours: int32 [16384, 8], P(('slab', 'brick')), may hold values from 0 to 191, as said below
- cell_index: int32 [16384, 128], P(('slab', 'brick')), may hold values from 0 to 32767
Outputs:
- arrived: float32 [32768, 6, 128], P(('slab', 'brick'))
- field_grid: float32 [10, 64, 256, 512], P(None, 'slab', 'brick')
The draws below stay inside these ranges and needn't reach their ends.
Inputs may be any that keep to these rules, and one draw needn't show every extreme that they name: `owners`: of the 64 blocks of one device, at most 4 name any one owner, and exactly 4 name some owner; in every slab one owner receives 4 blocks from every brick. `neighbours`: each row names 8 different places; never 64 plus the block's own place on its device; never a place below 64 on brick 0, nor one of 128 or more on the last brick.
All inputs are finite; a program needn't handle non-finite values.
Results may differ from the reference program's by a relative error of at most 0.00067.
Values sent between devices are 32-bit elements; how exact they have to be, the bound alone decides.
No kernel may reach another device: no remote copies, remote signals or barrier semaphores. Data moves between devices by JAX's collectives and lax.ppermute only.
A program may use at most 64 MiB of HBM per device.

```python
import math
import jax
import jax.numpy as jnp
from jax import lax

NB = 64
PB = 128
K = 8
FIELDS = 10
RAD = 3
CZ = 8
CY = 8
CX = 512
CAP = 4
BLOCKS = 16384
ARRIVED = 32768
CELLS = 32768
NZ = 64
NY = 256
NX = 512
N_SLAB = 8
N_BRICK = 32


def draw_owners(key, part):
    key = jax.random.fold_in(key, 11)
    first_key, second_key, third_key = jax.random.split(key, 3)
    device_count = N_SLAB * N_BRICK
    slot_count = N_BRICK * CAP
    hottest = jax.random.randint(first_key, (N_SLAB, 1, 1), 0, N_BRICK)
    hottest = jnp.broadcast_to(hottest, (N_SLAB, N_BRICK, 1)).reshape(device_count, 1)
    slot_owner = jnp.arange(slot_count, dtype=jnp.int32) // CAP
    ordering = jax.vmap(lambda k: jax.random.permutation(k, slot_count))(jax.random.split(second_key, device_count))
    scores = ordering.astype(jnp.int32) + jnp.where(slot_owner[None, :] == hottest, 0, slot_count)
    picked = jnp.argsort(scores, axis=1)[:, :NB]
    chosen = slot_owner[picked]
    shuffle = jax.vmap(lambda k: jax.random.permutation(k, NB))(jax.random.split(third_key, device_count))
    result = jnp.take_along_axis(chosen, shuffle, axis=1)
    return result.reshape(device_count * NB).astype(jnp.int32)


def draw_neighbours(key, part):
    key = jax.random.fold_in(key, 23)
    block_total = N_SLAB * N_BRICK * NB
    block_ids = jnp.arange(block_total, dtype=jnp.int32)
    brick_index = block_ids // NB % N_BRICK
    own_place = NB + block_ids % NB
    candidate = jnp.arange(3 * NB, dtype=jnp.int32)
    ordering = jax.vmap(lambda k: jax.random.permutation(k, 3 * NB))(jax.random.split(key, block_total)).astype(jnp.int32)
    barred = (candidate[None, :] == own_place[:, None]) | (candidate[None, :] < NB) & (brick_index[:, None] == 0) | (candidate[None, :] >= 2 * NB) & (brick_index[:, None] == N_BRICK - 1)
    scores = ordering + jnp.where(barred, 3 * NB, 0)
    return jnp.argsort(scores, axis=1)[:, :K].astype(jnp.int32)


def touch_ends(values, key, smallest, high):
    longest = values.shape.index(max(values.shape))
    spots = []
    for shift in (0, 1):
        where = [jax.random.randint(jax.random.fold_in(key, axis), (), 0, length) for axis, length in enumerate(values.shape)]
        where[longest] = (where[longest] + shift) % values.shape[longest]
        spots.append(tuple(where))
    return values.at[spots[0]].set(smallest).at[spots[1]].set(high)


def block_scale(key, dims, shards, smallest, largest):
    def one(axis_at, shards_of):
        steps = jax.random.uniform(jax.random.fold_in(jax.random.fold_in(key, 6), axis_at), (shards_of,), jnp.float32, smallest / len(shards), largest / len(shards))
        return jnp.repeat(jnp.exp(steps), dims[axis_at] // shards_of).reshape((-1,) + (1,) * (len(dims) - axis_at - 1))

    level = one(*shards[0])
    for cut in shards[1:]:
        level = level * one(*cut)
    return level


def normal_values(key, dims, scale, reach, cuts=(), kind=jnp.bfloat16):
    entries = scale * jax.random.normal(key, dims, jnp.float32)
    if cuts:
        entries = entries * block_scale(key, dims, cuts, -0.22, 0.18)
    return jnp.clip(entries, -reach, reach).astype(kind)


def setup_inputs(seed: int = 0) -> dict:
    key_list = jax.random.split(jax.random.key(seed), 7)
    positions = jnp.clip(9.0 * jax.random.uniform(key_list[0], (BLOCKS, 3, PB), jnp.float32) ** block_scale(key_list[0], (BLOCKS, 3, PB), ((0, 256),), -0.2, 0.2), 0.0, 9.0)
    velocities = normal_values(key_list[1], (BLOCKS, 3, PB), 1.0, 6.0, ((0, 256),), jnp.float32)
    radius = jnp.clip(0.35 + 0.29999998 * jax.random.uniform(key_list[2], (BLOCKS, PB), jnp.float32) ** block_scale(key_list[2], (BLOCKS, PB), ((0, 256),), -0.2, 0.2), 0.35, 0.65)
    owners = draw_owners(jax.random.fold_in(key_list[6], 71), 0)
    neighbours = draw_neighbours(jax.random.fold_in(key_list[6], 71), 0)
    cell_index = touch_ends(jax.random.randint(key_list[5], (BLOCKS, PB), 0, CELLS), jax.random.fold_in(key_list[5], 1), 0, CELLS - 1).astype(jnp.int32)
    return dict(positions=positions, velocities=velocities, radius=radius, owners=owners, neighbours=neighbours, cell_index=cell_index)


STIFFNESS = 1.0
TIMESTEP = 0.1
FLOOR_SQ = 0.0625
GRAVITY = (0.5, 0.0, -0.866)
COMPONENT_PAIRS = ((0, 0), (1, 1), (2, 2), (0, 1), (0, 2), (1, 2))

def pair_terms(own_blocks, others):
    offset = own_blocks[:, None, :3, :, None] - others[:, :, :3, None, :]
    offset_sq = lax.optimization_barrier(jnp.sum(offset * offset, axis=2))
    distance = jnp.sqrt(offset_sq + FLOOR_SQ)
    contact_reach = own_blocks[:, None, 3, :, None] + others[:, :, 3, None, :]
    intersection = jnp.maximum(contact_reach - distance, 0.0)
    push_scale = STIFFNESS * intersection / distance
    fabric_scale = intersection / (distance * distance)
    forces = lax.optimization_barrier(jnp.sum(push_scale[:, :, None] * offset, axis=(1, 4)))
    stress = jnp.stack([lax.optimization_barrier(jnp.sum(push_scale * offset[:, :, a] * offset[:, :, b], axis=(1, 3))) for a, b in COMPONENT_PAIRS], axis=1)
    fabric = jnp.stack([lax.optimization_barrier(jnp.sum(fabric_scale * offset[:, :, a] * offset[:, :, a], axis=(1, 3))) for a in range(3)], axis=1)
    return (forces, stress, fabric)

def advance_state(positions, velocities, radius, forces, stress, fabric):
    masses = 8.0 * radius * radius * radius
    gravity = jnp.array(GRAVITY, dtype=jnp.float32)[None, :, None]
    new_velocity = velocities + TIMESTEP * (forces / masses[:, None, :] + gravity)
    new_position = positions + TIMESTEP * new_velocity
    fields = jnp.concatenate([stress, masses[:, None, :], fabric], axis=1)
    rounded = lax.optimization_barrier(fields.astype(jnp.bfloat16)).astype(jnp.float32)
    return jnp.concatenate([new_position, new_velocity, rounded], axis=1)

def kernel_weights():
    gauss_raw = [math.exp(-(t * t) / 4.5) for t in range(-RAD, RAD + 1)]
    norm_total = sum(gauss_raw)
    return [v / norm_total for v in gauss_raw]

def blur(field_data, axis_dim, extent):
    weights = kernel_weights()
    result = weights[0] * lax.slice_in_dim(field_data, 0, extent, axis=axis_dim)
    for t in range(1, 2 * RAD + 1):
        result = result + weights[t] * lax.slice_in_dim(field_data, t, t + extent, axis=axis_dim)
    return result

def pad_axis(field_data, axis_dim):
    widths = [(0, 0)] * field_data.ndim
    widths[axis_dim] = (RAD, RAD)
    return jnp.pad(field_data, widths)

def reference(positions, velocities, radius, owners, neighbours, cell_index):
    block_total = positions.shape[0]
    device_count = N_SLAB * N_BRICK
    packed = jnp.concatenate([positions, radius[:, None, :]], axis=1)
    grouped = packed.reshape(N_SLAB, N_BRICK, NB, 4, PB)
    empty = jnp.zeros_like(grouped[:, :1])
    lower_side = jnp.concatenate([empty, grouped[:, :-1]], axis=1)
    upper_side = jnp.concatenate([grouped[:, 1:], empty], axis=1)
    extended = jnp.concatenate([lower_side, grouped, upper_side], axis=2).reshape(device_count, 3 * NB, 4, PB)
    block_ids = jnp.arange(block_total, dtype=jnp.int32)
    device = block_ids // NB
    own_place = NB + block_ids % NB
    chosen = jnp.concatenate([own_place[:, None], neighbours], axis=1)
    turns = block_total // 4

    def contact_group(inputs_pair):
        own_blocks, places, homes = inputs_pair
        others = extended[homes[:, None], places]
        return pair_terms(own_blocks, others)
    forces, stress, fabric = lax.map(contact_group, (packed.reshape(turns, 4, 4, PB), chosen.reshape(turns, 4, K + 1), device.reshape(turns, 4)))
    forces = forces.reshape(block_total, 3, PB)
    stress = stress.reshape(block_total, 6, PB)
    fabric = fabric.reshape(block_total, 3, PB)
    payload = advance_state(positions, velocities, radius, forces, stress, fabric)
    owner_hot = (owners[:, None] == jnp.arange(N_BRICK, dtype=jnp.int32)[None, :]).astype(jnp.int32).reshape(device_count, NB, N_BRICK)
    earlier = jnp.cumsum(owner_hot, axis=1) - owner_hot
    place_rank = lax.optimization_barrier(jnp.sum(earlier * owner_hot, axis=2)).reshape(block_total)
    slab_index = device // N_BRICK
    brick_index = device % N_BRICK
    target = ((slab_index * N_BRICK + owners) * N_BRICK + brick_index) * CAP + place_rank
    arrived_all = jnp.zeros((ARRIVED, 16, PB), jnp.float32).at[target].set(payload)
    arrived_cells = jnp.zeros((ARRIVED, PB), jnp.int32).at[target].set(cell_index)
    slot_count = N_BRICK * CAP
    receiver = jnp.arange(ARRIVED, dtype=jnp.int32) // slot_count
    segment = (receiver[:, None] * CELLS + arrived_cells).reshape(-1)
    values = jnp.transpose(arrived_all[:, 6:], (0, 2, 1)).reshape(-1, FIELDS)
    tile_sums = jax.ops.segment_sum(values, segment, num_segments=device_count * CELLS)
    tile_sums = tile_sums.reshape(N_SLAB, N_BRICK, CZ, CY, CX, FIELDS)
    tiles_grid = jnp.transpose(tile_sums, (5, 0, 2, 1, 3, 4)).reshape(FIELDS, NZ, NY, NX)
    smooth_x = blur(pad_axis(tiles_grid, 3), 3, NX)
    smooth_y = blur(pad_axis(smooth_x, 2), 2, NY)
    field_grid = blur(pad_axis(smooth_y, 1), 1, NZ)
    return (arrived_all[:, :6], field_grid)
```

```python
import math

import jax
import jax.numpy as jnp
from jax import lax
from jax.experimental import pallas as pl
from jax.experimental.pallas import tpu as pltpu
from jax.sharding import PartitionSpec as P

FIELDS = 10
RAD = 3
CZ = 8
CY = 8
CX = 512
CAP = 4
NB = 64
PB = 128
K = 8
BRICKS = 32
SLABS = 8
EARLY = 6
LATE = 12
FEAT = 32

TIMESTEP = 0.1
FLOOR_SQ = 0.0625
GRAVITY = (0.5, 0.0, -0.866)
PAIRS = ((0, 0), (1, 1), (2, 2), (0, 1), (0, 2), (1, 2))
CENTRE = 4.5
BF16 = jnp.bfloat16
F32 = jnp.float32


def kernel_weights():
    raw = [math.exp(-(t * t) / 4.5) for t in range(-RAD, RAD + 1)]
    total = sum(raw)
    return [v / total for v in raw]


def split3(value):
    high = value.astype(BF16).astype(F32)
    rest = value - high
    mid = rest.astype(BF16).astype(F32)
    return high, mid, rest - mid


def vmem():
    return pl.BlockSpec(memory_space=pltpu.VMEM)


def smem():
    return pl.BlockSpec(memory_space=pltpu.SMEM)


def clear_counts(counts):
    def clear(o, carry):
        counts[o] = 0
        return carry

    lax.fori_loop(0, BRICKS, clear, 0)


def next_slot(owners, counts, i):
    owner = owners[i]
    rank = counts[owner]
    counts[owner] = rank + 1
    return owner, rank


def early_kernel(owners, place, radius, cells, out, counts):
    clear_counts(counts)
    out[...] = jnp.zeros_like(out)

    def place_block(i, carry):
        owner, rank = next_slot(owners, counts, i)
        row = owner * (CAP * EARLY) + rank * EARLY
        for a in range(3):
            out[pl.ds(row + a, 1), :] = place[a, pl.ds(i, 1), :]
        out[pl.ds(row + 3, 1), :] = radius[pl.ds(i, 1), :]
        out[pl.ds(row + 4, 1), :] = cells[pl.ds(i, 1), :].astype(F32)
        return carry

    lax.fori_loop(0, NB, place_block, 0)


def early_payload(owners, place, radius, cells):
    return pl.pallas_call(
        early_kernel,
        out_shape=jax.ShapeDtypeStruct((BRICKS * CAP * EARLY, PB), F32),
        in_specs=[smem(), vmem(), vmem(), vmem()],
        out_specs=vmem(),
        scratch_shapes=[pltpu.SMEM((BRICKS,), jnp.int32)],
        name="early_payload",
    )(owners, place, radius, cells)


def contact_kernel(
    neighbours, owners, low, own, high, velocity, out, lane_masks, feat_rows, feat, own_feat, moment_rows, moments, sums, late, counts
):
    lane_group = lax.broadcasted_iota(jnp.int32, (PB, PB), 1) // FEAT
    for j in range(4):
        lane_masks[j] = jnp.where(lane_group == j, 1.0, 0.0).astype(BF16)
    for part, source in enumerate((low, own, high)):
        centred = [source[a] - CENTRE for a in range(3)]
        splits = [split3(c) for c in centred]
        norm = split3(centred[0] * centred[0] + centred[1] * centred[1] + centred[2] * centred[2])
        reach = split3(source[3])
        one = jnp.ones((NB, PB), F32)
        zero = jnp.zeros((NB, PB), F32)
        rows = []
        for h, m, l in splits:
            rows += [h, h, h, m, m, l]
        rows += [one] * 3 + list(norm) + list(reach)
        rows += [zero] * (FEAT - len(rows))
        for k, row in enumerate(rows):
            feat_rows[pl.ds(k, NB, stride=FEAT), :] = row

        for g in range(NB // 4):
            feat[part * (NB // 4) + g] = feat_rows[g * 128 : (g + 1) * 128, :].T.astype(BF16)
        x, y, z = centred
        basis = [x, y, z, x * x, y * y, z * z, x * y, x * z, y * z]
        parts = [split3(v) for v in basis]
        rows = [one] + [p[0] for p in parts] + [p[1] for p in parts] + [p[2] for p in parts]
        rows += [zero] * (FEAT - len(rows))
        for k, row in enumerate(rows):
            moment_rows[pl.ds(k, NB, stride=FEAT), :] = row
        for g in range(4):
            moments[pl.ds(part * NB + g * 16, 16)] = (
                moment_rows[g * 16 * FEAT : (g + 1) * 16 * FEAT, :].reshape(16, FEAT, PB).astype(BF16)
            )
        if part == 1:
            rows = []
            for h, m, l in splits:
                rows += [-2.0 * h, -2.0 * m, -2.0 * l, -2.0 * h, -2.0 * m, -2.0 * h]
            floored = split3(
                centred[0] * centred[0] + centred[1] * centred[1] + centred[2] * centred[2] + FLOOR_SQ
            )
            rows += list(floored) + [one] * 3
            rows += [zero] * (FEAT - len(rows))
            reach_rows = [zero] * 18 + list(reach) + [zero] * 3 + [one] * 3
            reach_rows += [zero] * (FEAT - len(reach_rows))
            for half, half_rows in enumerate((rows, reach_rows)):
                for k, row in enumerate(half_rows):
                    feat_rows[pl.ds(k, NB, stride=FEAT), :] = row
                for g in range(4):
                    own_feat[pl.ds(g * 16, 16), :, half * PB : (half + 1) * PB] = (
                        feat_rows[g * 16 * FEAT : (g + 1) * 16 * FEAT, :].reshape(16, FEAT, PB).astype(BF16)
                    )

    def block(i, carry):
        places = [NB + i] + [neighbours[i, k] for k in range(K)]
        weights = jnp.concatenate([own_feat[i]] * 4, axis=0)
        total = None
        for g in range(0, K + 1, 3):
            others = jnp.concatenate([feat[e >> 2] * lane_masks[e & 3] for e in places[g : g + 3]], axis=0)
            pair = jnp.dot(others, weights, preferred_element_type=F32)
            inverse = lax.rsqrt(pair[:, :PB])
            push = jnp.maximum(pair[:, PB:] * inverse - 1.0, 0.0)
            bend = push * inverse
            scales = jnp.concatenate([push.astype(BF16), bend.astype(BF16)], axis=1)
            basis = jnp.concatenate([moments[e] for e in places[g : g + 3]], axis=1)
            part = jnp.dot(basis, scales, preferred_element_type=F32)
            total = part if total is None else total + part
        sums[i] = total
        return carry

    lax.fori_loop(0, NB, block, 0, unroll=4)

    def summed(k, half):
        lanes = slice(half * PB, (half + 1) * PB)
        value = sums[:, k, lanes]
        if k:
            value = value + sums[:, k + 9, lanes] + sums[:, k + 18, lanes]
        return value

    centred = [own[a] - CENTRE for a in range(3)]
    weight = summed(0, 0)
    first = [summed(1 + a, 0) for a in range(3)]
    forces = [centred[a] * weight - first[a] for a in range(3)]
    results = []
    mass = 8.0 * own[3] * own[3] * own[3]
    for a in range(3):
        results.append(velocity[a] + TIMESTEP * (forces[a] / mass + GRAVITY[a]))
    for n, (a, b) in enumerate(PAIRS):
        results.append(
            (centred[a] * centred[b]) * weight - centred[a] * first[b] - centred[b] * first[a] + summed(4 + n, 0)
        )
    bent = summed(0, 1)
    for a in range(3):
        results.append(
            (centred[a] * centred[a]) * bent - 2.0 * (centred[a] * summed(1 + a, 1)) + summed(4 + a, 1)
        )
    for f, value in enumerate(results):
        late[f] = value

    clear_counts(counts)
    out[...] = jnp.zeros_like(out)

    def place_block(i, carry):
        owner, rank = next_slot(owners, counts, i)
        row = owner * (CAP * LATE) + rank * LATE
        for f in range(LATE):
            out[pl.ds(row + f, 1), :] = late[f, pl.ds(i, 1), :]
        return carry

    lax.fori_loop(0, NB, place_block, 0)


def contact_payload(neighbours, owners, low, own, high, velocity):
    return pl.pallas_call(
        contact_kernel,
        out_shape=jax.ShapeDtypeStruct((BRICKS * CAP * LATE, PB), F32),
        in_specs=[smem(), smem(), vmem(), vmem(), vmem(), vmem()],
        out_specs=vmem(),
        scratch_shapes=[
            pltpu.VMEM((4, PB, PB), BF16),
            pltpu.VMEM((NB * FEAT, PB), F32),
            pltpu.VMEM((3 * NB // 4, PB, PB), BF16),
            pltpu.VMEM((NB, FEAT, 2 * PB), BF16),
            pltpu.VMEM((NB * FEAT, PB), F32),
            pltpu.VMEM((3 * NB, FEAT, PB), BF16),
            pltpu.VMEM((NB, FEAT, 2 * PB), F32),
            pltpu.VMEM((LATE, NB, PB), F32),
            pltpu.SMEM((BRICKS,), jnp.int32),
        ],
        compiler_params=pltpu.CompilerParams(vmem_limit_bytes=40 * 1024 * 1024),
        cost_estimate=pl.CostEstimate(flops=20_000_000_000, bytes_accessed=8_000_000, transcendentals=9_437_184),
        name="contact_payload",
    )(neighbours, owners, low, own, high, velocity)


def tap(distance):
    weights = kernel_weights()
    value = jnp.zeros(distance.shape, F32)
    for t in range(RAD + 1):
        value = jnp.where(jnp.abs(distance) == t, weights[RAD + t], value)
    return value


def split2(value):
    high = value.astype(BF16)
    return high, (value - high.astype(F32)).astype(BF16)


def deposit_kernel(even, early, late, arrived, tile, send_a, send_b, grid):
    grid[...] = jnp.zeros_like(grid)
    group = 2
    width = group * CAP * PB

    def chunk(c, carry):
        slots = [(c * group + s, q) for s in range(group) for q in range(CAP)]
        cells = jnp.concatenate(
            [early[s, EARLY * q + 4 : EARLY * q + 5, :] for s, q in slots], axis=1
        ).astype(jnp.int32)
        reach = jnp.concatenate([early[s, EARLY * q + 3 : EARLY * q + 4, :] for s, q in slots], axis=1)
        mass = 8.0 * reach * reach * reach
        rest = jnp.concatenate([late[s, LATE * q + 3 : LATE * q + 12, :] for s, q in slots], axis=1)
        fields = jnp.concatenate([rest[:6], mass, rest[6:9]], axis=0)
        across = lax.broadcasted_iota(jnp.int32, (CZ * CY, width), 0) == cells // CX
        along = jnp.where(
            lax.broadcasted_iota(jnp.int32, (CX, width), 0) == cells % CX, 1.0, 0.0
        ).astype(BF16)
        weighted = jnp.concatenate(
            [jnp.where(across, fields[f : f + 1], 0.0).astype(BF16) for f in range(FIELDS)], axis=0
        )
        grid[...] += lax.dot_general(
            weighted, along, (((1,), (1,)), ((), ())), preferred_element_type=F32
        )
        return carry

    lax.fori_loop(0, BRICKS // group, chunk, 0)

    def arrive(s, carry):
        for q in range(CAP):
            velocity = late[s, LATE * q : LATE * q + 3, :]
            arrived[s * CAP + q, 3:6, :] = velocity
            arrived[s * CAP + q, 0:3, :] = early[s, EARLY * q : EARLY * q + 3, :] + TIMESTEP * velocity
        return carry

    lax.fori_loop(0, BRICKS, arrive, 0)
    rows = lax.broadcasted_iota(jnp.int32, (CX, CX), 0)
    band_high, band_low = split2(tap(rows - lax.broadcasted_iota(jnp.int32, (CX, CX), 1)))

    def smooth(f, carry):
        high, low = split2(grid[pl.ds(pl.multiple_of(f * CZ * CY, CZ * CY), CZ * CY), :])
        value = jnp.dot(jnp.concatenate([high, low], axis=0), band_high, preferred_element_type=F32)
        tile[f] = value[: CZ * CY] + value[CZ * CY :] + jnp.dot(high, band_low, preferred_element_type=F32)
        return carry

    lax.fori_loop(0, FIELDS, smooth, 0)

    def border(target, first):
        for f in range(FIELDS):
            for z in range(CZ):
                target[f, z * RAD : (z + 1) * RAD, :] = tile[f, z * CY + first : z * CY + first + RAD, :]

    @pl.when(even[0] == 1)
    def _():
        border(send_a, CY - RAD)
        border(send_b, 0)

    @pl.when(even[0] == 0)
    def _():
        border(send_a, 0)
        border(send_b, CY - RAD)


def deposit(even, early, late):
    side = jax.ShapeDtypeStruct((FIELDS, CZ * RAD, CX), F32)
    return pl.pallas_call(
        deposit_kernel,
        out_shape=(
            jax.ShapeDtypeStruct((BRICKS * CAP, 6, PB), F32),
            jax.ShapeDtypeStruct((FIELDS, CZ * CY, CX), F32),
            side,
            side,
        ),
        in_specs=[smem(), vmem(), vmem()],
        out_specs=(vmem(), vmem(), vmem(), vmem()),
        scratch_shapes=[pltpu.VMEM((FIELDS * CZ * CY, CX), F32)],
        compiler_params=pltpu.CompilerParams(vmem_limit_bytes=40 * 1024 * 1024),
        cost_estimate=pl.CostEstimate(flops=12_000_000_000, bytes_accessed=8_000_000, transcendentals=0),
        name="deposit",
    )(even, early, late)


def halo_weights(even, along_rows):
    def line(value):
        return value % CY if along_rows else value // CY

    def other(value):
        return value // CY if along_rows else value % CY

    def side_line(value):
        return value % RAD if along_rows else value // CY

    def side_other(value):
        return value // RAD if along_rows else value % CY

    def part(count, place, same):
        out = lax.broadcasted_iota(jnp.int32, (CZ * CY, count), 0)
        source = lax.broadcasted_iota(jnp.int32, (CZ * CY, count), 1)
        return jnp.where(other(out) == same(source), tap(place(source) - line(out)), 0.0)

    above = RAD * CY
    return jnp.concatenate(
        [
            part(CZ * CY, line, other),
            part(above, lambda v: side_line(v) + jnp.where(even == 1, CY, -RAD), side_other),
            part(above, lambda v: side_line(v) + jnp.where(even == 1, -RAD, CY), side_other),
        ],
        axis=1,
    )


def smooth_all(weights, tile, side_a, side_b, out):
    weight_high, weight_low = split2(weights)
    both = jnp.concatenate([weight_high, weight_low], axis=0)
    rows = CZ * CY

    def smooth(f, carry):
        value = jnp.concatenate([tile[f], side_a[f], side_b[f]], axis=0)
        high, low = split2(value)
        part = jnp.dot(both, high, preferred_element_type=F32)
        result = part[:rows] + part[rows:] + jnp.dot(weight_high, low, preferred_element_type=F32)
        out[f] = result.reshape(out.shape[1:])
        return carry

    lax.fori_loop(0, FIELDS, smooth, 0, unroll=2)


def smooth_rows_kernel(even, slab_even, tile, side_a, side_b, out, send_a, send_b):
    smooth_all(halo_weights(even[0], True), tile, side_a, side_b, out)
    rows = RAD * CY
    top = CZ * CY - rows

    @pl.when(slab_even[0] == 1)
    def _():
        send_a[...] = out[:, top:, :]
        send_b[...] = out[:, :rows, :]

    @pl.when(slab_even[0] == 0)
    def _():
        send_a[...] = out[:, :rows, :]
        send_b[...] = out[:, top:, :]


def smooth_rows(even, slab_even, tile, side_a, side_b):
    side = jax.ShapeDtypeStruct((FIELDS, CY * RAD, CX), F32)
    return pl.pallas_call(
        smooth_rows_kernel,
        out_shape=(jax.ShapeDtypeStruct((FIELDS, CZ * CY, CX), F32), side, side),
        in_specs=[smem(), smem(), vmem(), vmem(), vmem()],
        out_specs=(vmem(), vmem(), vmem()),
        compiler_params=pltpu.CompilerParams(vmem_limit_bytes=40 * 1024 * 1024),
        name="smooth_rows",
    )(even, slab_even, tile, side_a, side_b)


def smooth_layers_kernel(slab_even, tile, side_a, side_b, out):
    smooth_all(halo_weights(slab_even[0], False), tile, side_a, side_b, out)


def smooth_layers(slab_even, tile, side_a, side_b):
    return pl.pallas_call(
        smooth_layers_kernel,
        out_shape=jax.ShapeDtypeStruct((FIELDS, CZ, CY, CX), F32),
        in_specs=[smem(), vmem(), vmem(), vmem()],
        out_specs=vmem(),
        compiler_params=pltpu.CompilerParams(vmem_limit_bytes=40 * 1024 * 1024),
        name="smooth_layers",
    )(slab_even, tile, side_a, side_b)


def swap_near(value, axis, count):
    return lax.ppermute(value, axis, [(i, i ^ 1) for i in range(count)])


def swap_far(value, axis, count):
    return lax.ppermute(value, axis, [(i, i + 1 if i % 2 else i - 1) for i in range(1, count - 1)])


def body(positions, velocities, radius, owners, neighbours, cell_index):
    brick, slab = lax.axis_index("brick"), lax.axis_index("slab")
    even = (1 - brick % 2).astype(jnp.int32)
    slab_even = (1 - slab % 2).astype(jnp.int32).reshape(1)
    place = jnp.transpose(positions, (1, 0, 2))
    velocity = jnp.transpose(velocities, (1, 0, 2))
    packed = jnp.concatenate([place, radius[None]], axis=0)
    early = early_payload(owners, place, radius, cell_index)
    early = lax.all_to_all(
        early.reshape(BRICKS, CAP * EARLY, PB), "brick", split_axis=0, concat_axis=0, tiled=True
    )
    near = swap_near(packed, "brick", BRICKS)
    far = swap_far(packed, "brick", BRICKS)
    swapped = jnp.where(neighbours < NB, neighbours + 2 * NB, jnp.where(neighbours >= 2 * NB, neighbours - 2 * NB, neighbours))
    places = jnp.where(even == 1, swapped, neighbours)
    late = contact_payload(places, owners, near, packed, far, velocity)
    late = lax.all_to_all(
        late.reshape(BRICKS, CAP * LATE, PB), "brick", split_axis=0, concat_axis=0, tiled=True
    )
    even = even.reshape(1)
    arrived, tile, send_a, send_b = deposit(even, early, late)
    side_a = swap_near(send_a, "brick", BRICKS)
    side_b = swap_far(send_b, "brick", BRICKS)
    rows, send_a, send_b = smooth_rows(even, slab_even, tile, side_a, side_b)
    side_a = swap_near(send_a, "slab", SLABS)
    side_b = swap_far(send_b, "slab", SLABS)
    return arrived, smooth_layers(slab_even, rows, side_a, side_b)


def solution(mesh):
    return jax.shard_map(
        body,
        mesh=mesh,
        in_specs=(
            P(("slab", "brick"), None, None),
            P(("slab", "brick"), None, None),
            P(("slab", "brick"), None),
            P(("slab", "brick")),
            P(("slab", "brick"), None),
            P(("slab", "brick"), None),
        ),
        out_specs=(P(("slab", "brick"), None, None), P(None, "slab", "brick", None)),
        check_vma=False,
    )
```

```python
import math

import jax
import jax.numpy as jnp
from jax import lax
from jax.experimental import pallas as pl
from jax.experimental.pallas import tpu as pltpu
from jax.sharding import PartitionSpec as P

FIELDS = 10
RAD = 3
CZ = 8
CY = 8
CX = 512
CAP = 4
NB = 64
PB = 128
K = 8
BRICKS = 32
SLABS = 8
TILE = 8
REST = 40
FIRST = 6
SECOND = 4
FEAT = 32

TIMESTEP = 0.1
FLOOR_SQ = 0.0625
GRAVITY = (0.5, 0.0, -0.866)
PAIRS = ((0, 0), (1, 1), (2, 2), (0, 1), (0, 2), (1, 2))
CENTRE = 4.5
BF16 = jnp.bfloat16
F32 = jnp.float32


def kernel_weights():
    raw = [math.exp(-(t * t) / 4.5) for t in range(-RAD, RAD + 1)]
    total = sum(raw)
    return [v / total for v in raw]


def split3(value):
    high = value.astype(BF16).astype(F32)
    rest = value - high
    mid = rest.astype(BF16).astype(F32)
    return high, mid, rest - mid


def vmem():
    return pl.BlockSpec(memory_space=pltpu.VMEM)


def smem():
    return pl.BlockSpec(memory_space=pltpu.SMEM)


def clear_counts(counts):
    def clear(o, carry):
        counts[o] = 0
        return carry

    lax.fori_loop(0, BRICKS, clear, 0)


def next_slot(owners, counts, i):
    owner = owners[i]
    rank = counts[owner]
    counts[owner] = rank + 1
    return owner, rank


def contact_kernel(
    even,
    neighbours_in,
    owners_in,
    near,
    own,
    far,
    velocity_in,
    cells_in,
    out,
    out_rest,
    lane_masks,
    feat_rows,
    feat,
    own_feat,
    moment_rows,
    moments,
    sums,
    ready,
    rest,
    last,
    counts,
    neighbours,
    owners,
    velocity,
    cells,
    copy_sems,
):
    lane_group = lax.broadcasted_iota(jnp.int32, (PB, PB), 1) // FEAT
    for j in range(4):
        lane_masks[j] = jnp.where(lane_group == j, 1.0, 0.0).astype(BF16)
    copies = [
        pltpu.make_async_copy(source, target, copy_sems.at[n])
        for n, (source, target) in enumerate(
            ((neighbours_in, neighbours), (owners_in, owners), (velocity_in, velocity), (cells_in, cells))
        )
    ]
    for copy in copies:
        copy.start()
    near_part = 2 * even[0]
    for part, source in ((near_part, near), (1, own), (2 - near_part, far)):
        centred = [source[a] - CENTRE for a in range(3)]
        splits = [split3(c) for c in centred]
        norm = split3(centred[0] * centred[0] + centred[1] * centred[1] + centred[2] * centred[2])
        reach = split3(source[3])
        one = jnp.ones((NB, PB), F32)
        zero = jnp.zeros((NB, PB), F32)
        rows = []
        for h, m, l in splits:
            rows += [h, h, h, m, m, l]
        rows += [one] * 3 + list(norm) + list(reach)
        rows += [zero] * (FEAT - len(rows))
        for k, row in enumerate(rows):
            feat_rows[pl.ds(k, NB, stride=FEAT), :] = row

        for g in range(NB // 4):
            feat[part * (NB // 4) + g] = feat_rows[g * 128 : (g + 1) * 128, :].T.astype(BF16)
        x, y, z = centred
        basis = [x, y, z, x * x, y * y, z * z, x * y, x * z, y * z]
        parts = [split3(v) for v in basis]
        rows = [one] + [p[0] for p in parts] + [p[1] for p in parts] + [p[2] for p in parts]
        rows += [zero] * (FEAT - len(rows))
        for k, row in enumerate(rows):
            moment_rows[pl.ds(k, NB, stride=FEAT), :] = row
        for g in range(4):
            moments[pl.ds(part * NB + g * 16, 16)] = (
                moment_rows[g * 16 * FEAT : (g + 1) * 16 * FEAT, :].reshape(16, FEAT, PB).astype(BF16)
            )
        if source is own:
            rows = []
            for h, m, l in splits:
                rows += [-2.0 * h, -2.0 * m, -2.0 * l, -2.0 * h, -2.0 * m, -2.0 * h]
            floored = split3(
                centred[0] * centred[0] + centred[1] * centred[1] + centred[2] * centred[2] + FLOOR_SQ
            )
            rows += list(floored) + [one] * 3
            rows += [zero] * (FEAT - len(rows))
            reach_rows = [zero] * 18 + list(reach) + [zero] * 3 + [one] * 3
            reach_rows += [zero] * (FEAT - len(reach_rows))
            for half, half_rows in enumerate((rows, reach_rows)):
                for k, row in enumerate(half_rows):
                    feat_rows[pl.ds(k, NB, stride=FEAT), :] = row
                for g in range(4):
                    own_feat[pl.ds(g * 16, 16), :, half * PB : (half + 1) * PB] = (
                        feat_rows[g * 16 * FEAT : (g + 1) * 16 * FEAT, :].reshape(16, FEAT, PB).astype(BF16)
                    )

    copies[0].wait()

    def block(i, carry):
        places = [NB + i] + [neighbours[k, i] for k in range(K)]
        weights = jnp.concatenate([own_feat[i]] * 4, axis=0)
        total = None
        for g in range(0, K + 1, 3):
            others = jnp.concatenate([feat[e >> 2] * lane_masks[e & 3] for e in places[g : g + 3]], axis=0)
            pair = jnp.dot(others, weights, preferred_element_type=F32)
            inverse = lax.rsqrt(pair[:, :PB])
            push = jnp.maximum(pair[:, PB:] * inverse - 1.0, 0.0)
            bend = push * inverse
            scales = jnp.concatenate([push.astype(BF16), bend.astype(BF16)], axis=1)
            basis = jnp.concatenate([moments[e] for e in places[g : g + 3]], axis=1)
            part = jnp.dot(basis, scales, preferred_element_type=F32)
            total = part if total is None else total + part
        sums[i] = total
        return carry

    lax.fori_loop(0, NB, block, 0, unroll=8)

    for copy in copies[1:]:
        copy.wait()

    def summed(k, half):
        lanes = slice(half * PB, (half + 1) * PB)
        value = sums[:, k, lanes]
        if k:
            value = value + sums[:, k + 9, lanes] + sums[:, k + 18, lanes]
        return value

    centred = [own[a] - CENTRE for a in range(3)]
    weight = summed(0, 0)
    first = [summed(1 + a, 0) for a in range(3)]
    forces = [centred[a] * weight - first[a] for a in range(3)]
    mass = 8.0 * own[3] * own[3] * own[3]
    results = []
    for n, (a, b) in enumerate(PAIRS):
        results.append(
            (centred[a] * centred[b]) * weight - centred[a] * first[b] - centred[b] * first[a] + summed(4 + n, 0)
        )
    for f, value in enumerate(results + [own[3], cells[...].astype(F32)]):
        ready[pl.ds(f, NB, stride=TILE), :] = value

    moved = [velocity[a] + TIMESTEP * (forces[a] / mass + GRAVITY[a]) for a in range(3)]
    bent = summed(0, 1)
    fabric = [
        (centred[a] * centred[a]) * bent - 2.0 * (centred[a] * summed(1 + a, 1)) + summed(4 + a, 1)
        for a in range(3)
    ]
    state = [own[a] + TIMESTEP * moved[a] for a in range(3)] + moved + fabric[:2]
    for f, value in enumerate(state):
        rest[pl.ds(f, NB, stride=TILE), :] = value
    last[...] = fabric[2]

    clear_counts(counts)
    out[...] = jnp.zeros_like(out)
    out_rest[...] = jnp.zeros_like(out_rest)

    def place_block(i, carry):
        owner, rank = next_slot(owners, counts, i)
        here = pl.ds(pl.multiple_of(i * TILE, TILE), TILE)
        slot = pl.multiple_of((owner * CAP + rank) * TILE, TILE)
        out[pl.ds(slot, TILE), :] = ready[here, :]
        out_rest[pl.ds(pl.multiple_of(owner * REST + rank * TILE, TILE), TILE), :] = rest[here, :]
        out_rest[pl.ds(owner * REST + CAP * TILE + rank, 1), :] = last[pl.ds(i, 1), :]
        return carry

    lax.fori_loop(0, NB, place_block, 0, unroll=4)


def contact(even, neighbours, owners, near, own, far, velocity, cells):
    anywhere = pl.BlockSpec(memory_space=pl.ANY)
    return pl.pallas_call(
        contact_kernel,
        out_shape=(
            jax.ShapeDtypeStruct((BRICKS * CAP * TILE, PB), F32),
            jax.ShapeDtypeStruct((BRICKS * REST, PB), F32),
        ),
        in_specs=[smem(), anywhere, anywhere, vmem(), vmem(), vmem(), anywhere, anywhere],
        out_specs=(vmem(), vmem()),
        scratch_shapes=[
            pltpu.VMEM((4, PB, PB), BF16),
            pltpu.VMEM((NB * FEAT, PB), F32),
            pltpu.VMEM((3 * NB // 4, PB, PB), BF16),
            pltpu.VMEM((NB, FEAT, 2 * PB), BF16),
            pltpu.VMEM((NB * FEAT, PB), F32),
            pltpu.VMEM((3 * NB, FEAT, PB), BF16),
            pltpu.VMEM((NB, FEAT, 2 * PB), F32),
            pltpu.VMEM((NB * TILE, PB), F32),
            pltpu.VMEM((NB * TILE, PB), F32),
            pltpu.VMEM((NB, PB), F32),
            pltpu.SMEM((BRICKS,), jnp.int32),
            pltpu.SMEM((K, NB), jnp.int32),
            pltpu.SMEM((NB,), jnp.int32),
            pltpu.VMEM((3, NB, PB), F32),
            pltpu.VMEM((NB, PB), jnp.int32),
            pltpu.SemaphoreType.DMA((4,)),
        ],
        compiler_params=pltpu.CompilerParams(vmem_limit_bytes=62 * 1024 * 1024),
        cost_estimate=pl.CostEstimate(flops=20_000_000_000, bytes_accessed=8_000_000, transcendentals=9_437_184),
        name="contact",
    )(even, neighbours, owners, near, own, far, velocity, cells)


def tap(distance):
    weights = kernel_weights()
    value = jnp.zeros(distance.shape, F32)
    for t in range(RAD + 1):
        value = jnp.where(jnp.abs(distance) == t, weights[RAD + t], value)
    return value


def split2(value):
    high = value.astype(BF16)
    return high, (value - high.astype(F32)).astype(BF16)


def deposit_grid(grid, chunk_fields, early):
    grid[...] = jnp.zeros_like(grid)
    group = 8
    width = group * CAP * PB

    def chunk(c, carry):
        slots = [(c * group + s, q) for s in range(group) for q in range(CAP)]
        first = jnp.concatenate([early[s, TILE * q : TILE * (q + 1), :] for s, q in slots], axis=1)
        fields = chunk_fields(first, slots)
        cells = first[7:8].astype(jnp.int32)
        across = lax.broadcasted_iota(jnp.int32, (CZ * CY, width), 0) == cells // CX
        along = jnp.where(
            lax.broadcasted_iota(jnp.int32, (CX, width), 0) == cells % CX, 1.0, 0.0
        ).astype(BF16)
        weighted = jnp.concatenate(
            [jnp.where(across, field, 0.0).astype(BF16) for field in fields], axis=0
        )
        grid[...] += lax.dot_general(
            weighted, along, (((1,), (1,)), ((), ())), preferred_element_type=F32
        )
        return carry

    lax.fori_loop(0, BRICKS // group, chunk, 0)


def smooth_columns(slab_even, grid, tile, send_a, send_b):
    count = tile.shape[0]
    rows = lax.broadcasted_iota(jnp.int32, (CX, CX), 0)
    band_high, band_low = split2(tap(rows - lax.broadcasted_iota(jnp.int32, (CX, CX), 1)))

    def smooth(f, carry):
        high, low = split2(grid[pl.ds(pl.multiple_of(f * CZ * CY, CZ * CY), CZ * CY), :])
        value = jnp.dot(jnp.concatenate([high, low], axis=0), band_high, preferred_element_type=F32)
        tile[f] = value[: CZ * CY] + value[CZ * CY :] + jnp.dot(high, band_low, preferred_element_type=F32)
        return carry

    lax.fori_loop(0, count, smooth, 0, unroll=2)

    rows = RAD * CY
    top = CZ * CY - rows

    @pl.when(slab_even[0] == 1)
    def _():
        send_a[...] = tile[:, top:, :]
        send_b[...] = tile[:, :rows, :]

    @pl.when(slab_even[0] == 0)
    def _():
        send_a[...] = tile[:, :rows, :]
        send_b[...] = tile[:, top:, :]


def deposit_first_kernel(slab_even, early, tile, send_a, send_b, grid):
    deposit_grid(grid, lambda first, slots: [first[f : f + 1] for f in range(FIRST)], early)
    smooth_columns(slab_even, grid, tile, send_a, send_b)


def deposit_second_kernel(slab_even, early, late, tile, send_a, send_b, grid):
    def fields(first, slots):
        reach = first[6:7]
        fabric = jnp.concatenate([late[s, TILE * q + 6 : TILE * q + 8, :] for s, q in slots], axis=1)
        last = jnp.concatenate([late[s, CAP * TILE + q : CAP * TILE + q + 1, :] for s, q in slots], axis=1)
        return [8.0 * reach * reach * reach, fabric[:1], fabric[1:], last]

    deposit_grid(grid, fields, early)
    smooth_columns(slab_even, grid, tile, send_a, send_b)


def deposit(kernel, count, name, slab_even, *parts):
    side = jax.ShapeDtypeStruct((count, CZ * RAD, CX), F32)
    return pl.pallas_call(
        kernel,
        out_shape=(jax.ShapeDtypeStruct((count, CZ * CY, CX), F32), side, side),
        in_specs=[smem()] + [vmem()] * len(parts),
        out_specs=(vmem(), vmem(), vmem()),
        scratch_shapes=[pltpu.VMEM((count * CZ * CY, CX), F32)],
        compiler_params=pltpu.CompilerParams(vmem_limit_bytes=40 * 1024 * 1024),
        cost_estimate=pl.CostEstimate(flops=count * 1_200_000_000, bytes_accessed=4_000_000, transcendentals=0),
        name=name,
    )(slab_even, *parts)


def halo_weights(even, along_rows):
    def line(value):
        return value % CY if along_rows else value // CY

    def other(value):
        return value // CY if along_rows else value % CY

    def side_line(value):
        return value % RAD if along_rows else value // CY

    def side_other(value):
        return value // RAD if along_rows else value % CY

    def part(count, place, same):
        out = lax.broadcasted_iota(jnp.int32, (CZ * CY, count), 0)
        source = lax.broadcasted_iota(jnp.int32, (CZ * CY, count), 1)
        return jnp.where(other(out) == same(source), tap(place(source) - line(out)), 0.0)

    above = RAD * CY
    return jnp.concatenate(
        [
            part(CZ * CY, line, other),
            part(above, lambda v: side_line(v) + jnp.where(even == 1, CY, -RAD), side_other),
            part(above, lambda v: side_line(v) + jnp.where(even == 1, -RAD, CY), side_other),
        ],
        axis=1,
    )


def smooth_all(weights, tile, side_a, side_b, out, first=0):
    weight_high, weight_low = split2(weights)
    both = jnp.concatenate([weight_high, weight_low], axis=0)
    rows = CZ * CY

    def smooth(f, carry):
        value = jnp.concatenate([tile[f], side_a[f], side_b[f]], axis=0)
        high, low = split2(value)
        part = jnp.dot(both, high, preferred_element_type=F32)
        result = part[:rows] + part[rows:] + jnp.dot(weight_high, low, preferred_element_type=F32)
        out[first + f] = result.reshape(out.shape[1:])
        return carry

    lax.fori_loop(0, tile.shape[0], smooth, 0, unroll=2)


def smooth_layers_kernel(even, slab_even, tile, side_a, side_b, out, send_a, send_b):
    smooth_all(halo_weights(slab_even[0], False), tile, side_a, side_b, out)

    def border(target, first):
        for f in range(tile.shape[0]):
            for z in range(CZ):
                target[f, z * RAD : (z + 1) * RAD, :] = out[f, z * CY + first : z * CY + first + RAD, :]

    @pl.when(even[0] == 1)
    def _():
        border(send_a, CY - RAD)
        border(send_b, 0)

    @pl.when(even[0] == 0)
    def _():
        border(send_a, 0)
        border(send_b, CY - RAD)


def smooth_layers(even, slab_even, tile, side_a, side_b):
    count = tile.shape[0]
    side = jax.ShapeDtypeStruct((count, CZ * RAD, CX), F32)
    return pl.pallas_call(
        smooth_layers_kernel,
        out_shape=(jax.ShapeDtypeStruct((count, CZ * CY, CX), F32), side, side),
        in_specs=[smem(), smem(), vmem(), vmem(), vmem()],
        out_specs=(vmem(), vmem(), vmem()),
        compiler_params=pltpu.CompilerParams(vmem_limit_bytes=40 * 1024 * 1024),
        name="smooth_layers",
    )(even, slab_even, tile, side_a, side_b)


def smooth_rows_kernel(even, tile, side_a, side_b, tile2, side_a2, side_b2, out):
    weights = halo_weights(even[0], True)
    smooth_all(weights, tile, side_a, side_b, out)
    smooth_all(weights, tile2, side_a2, side_b2, out, FIRST)


def smooth_rows(even, *parts):
    return pl.pallas_call(
        smooth_rows_kernel,
        out_shape=jax.ShapeDtypeStruct((FIELDS, CZ, CY, CX), F32),
        in_specs=[smem()] + [vmem()] * len(parts),
        out_specs=vmem(),
        compiler_params=pltpu.CompilerParams(vmem_limit_bytes=40 * 1024 * 1024),
        name="smooth_rows",
    )(even, *parts)


def swap_near(value, axis, count):
    return lax.ppermute(value, axis, [(i, i ^ 1) for i in range(count)])


def swap_far(value, axis, count):
    return lax.ppermute(value, axis, [(i, i + 1 if i % 2 else i - 1) for i in range(1, count - 1)])


def to_owners(value):
    return lax.all_to_all(value.reshape(BRICKS, -1, PB), "brick", split_axis=0, concat_axis=0, tiled=True)


def swap_layers(even, slab_even, tile, send_a, send_b):
    side_a = swap_near(send_a, "slab", SLABS)
    side_b = swap_far(send_b, "slab", SLABS)
    return smooth_layers(even, slab_even, tile, side_a, side_b)


def swap_rows(layers, send_a, send_b):
    return layers, swap_near(send_a, "brick", BRICKS), swap_far(send_b, "brick", BRICKS)


def body(positions, velocities, radius, owners, neighbours, cell_index):
    even = (1 - (lax.axis_index("brick") & 1)).astype(jnp.int32).reshape(1)
    slab_even = (1 - (lax.axis_index("slab") & 1)).astype(jnp.int32).reshape(1)
    velocity = jnp.transpose(velocities, (1, 0, 2))
    packed = jnp.concatenate([jnp.transpose(positions, (1, 0, 2)), radius[None]], axis=0)
    near = swap_near(packed, "brick", BRICKS)
    far = swap_far(packed, "brick", BRICKS)
    first, rest = contact(even, neighbours.T, owners, near, packed, far, velocity, cell_index)
    first = to_owners(first)
    rest = to_owners(rest)
    tiles = deposit(deposit_first_kernel, FIRST, "deposit_first", slab_even, first)
    tiles2 = deposit(deposit_second_kernel, SECOND, "deposit_second", slab_even, first, rest)
    parts = swap_rows(*swap_layers(even, slab_even, *tiles))
    parts2 = swap_rows(*swap_layers(even, slab_even, *tiles2))
    arrived = rest[:, : CAP * TILE].reshape(BRICKS * CAP, TILE, PB)[:, :6]
    return arrived, smooth_rows(even, *parts, *parts2)


def solution(mesh):
    return jax.shard_map(
        body,
        mesh=mesh,
        in_specs=(
            P(("slab", "brick"), None, None),
            P(("slab", "brick"), None, None),
            P(("slab", "brick"), None),
            P(("slab", "brick")),
            P(("slab", "brick"), None),
            P(("slab", "brick"), None),
        ),
        out_specs=(P(("slab", "brick"), None, None), P(None, "slab", "brick", None)),
        check_vma=False,
    )
```

```python
import math

import jax
import jax.numpy as jnp
from jax import lax
from jax.experimental import pallas as pl
from jax.experimental.pallas import tpu as pltpu
from jax.sharding import PartitionSpec as P

FIELDS = 10
RAD = 3
CZ = 8
CY = 8
CX = 512
CAP = 4
NB = 64
PB = 128
K = 8
BRICKS = 32
SLABS = 8
TILE = 8
REST = 40
FIRST = 6
SECOND = 4
FEAT = 32
GROUP = 3

TIMESTEP = 0.1
FLOOR_SQ = 0.0625
GRAVITY = (0.5, 0.0, -0.866)
PAIRS = ((0, 0), (1, 1), (2, 2), (0, 1), (0, 2), (1, 2))
CENTRE = 4.5
BF16 = jnp.bfloat16
F32 = jnp.float32


def kernel_weights():
    raw = [math.exp(-(t * t) / 4.5) for t in range(-RAD, RAD + 1)]
    total = sum(raw)
    return [v / total for v in raw]


def split3(value):
    high = value.astype(BF16).astype(F32)
    rest = value - high
    mid = rest.astype(BF16).astype(F32)
    return high, mid, rest - mid


def vmem():
    return pl.BlockSpec(memory_space=pltpu.VMEM)


def smem():
    return pl.BlockSpec(memory_space=pltpu.SMEM)


def clear_counts(counts):
    def clear(o, carry):
        counts[o] = 0
        return carry

    lax.fori_loop(0, BRICKS, clear, 0)


def next_slot(owners, counts, i):
    owner = owners[i]
    rank = counts[owner]
    counts[owner] = rank + 1
    return owner, rank


def contact_kernel(
    even,
    neighbours_in,
    owners_in,
    near,
    own,
    far,
    velocity_in,
    cells_in,
    out,
    out_rest,
    lane_masks,
    feat_rows,
    feat,
    own_feat,
    moment_rows,
    moments,
    sums,
    ready,
    rest,
    last,
    counts,
    neighbours,
    owners,
    velocity,
    cells,
    copy_sems,
    scales_even,
    scales_odd,
):
    lane_group = lax.broadcasted_iota(jnp.int32, (PB, PB), 1) // FEAT
    for j in range(4):
        lane_masks[j] = jnp.where(lane_group == j, 1.0, 0.0).astype(BF16)
    copies = [
        pltpu.make_async_copy(source, target, copy_sems.at[n])
        for n, (source, target) in enumerate(
            ((neighbours_in, neighbours), (owners_in, owners), (velocity_in, velocity), (cells_in, cells))
        )
    ]
    for copy in copies:
        copy.start()
    near_part = 2 * even[0]
    for part, source in ((near_part, near), (1, own), (2 - near_part, far)):
        centred = [source[a] - CENTRE for a in range(3)]
        splits = [split3(c) for c in centred]
        norm = split3(centred[0] * centred[0] + centred[1] * centred[1] + centred[2] * centred[2])
        reach = split3(source[3])
        one = jnp.ones((NB, PB), F32)
        zero = jnp.zeros((NB, PB), F32)
        rows = []
        for h, m, l in splits:
            rows += [h, h, h, m, m, l]
        rows += [one] * 3 + list(norm) + list(reach)
        rows += [zero] * (FEAT - len(rows))
        for k, row in enumerate(rows):
            feat_rows[pl.ds(k, NB, stride=FEAT), :] = row

        for g in range(NB // 4):
            feat[part * (NB // 4) + g] = feat_rows[g * 128 : (g + 1) * 128, :].T.astype(BF16)
        x, y, z = centred
        basis = [x, y, z, x * x, y * y, z * z, x * y, x * z, y * z]
        parts = [split3(v) for v in basis]
        rows = [one] + [p[0] for p in parts] + [p[1] for p in parts] + [p[2] for p in parts]
        rows += [zero] * (FEAT - len(rows))
        for k, row in enumerate(rows):
            moment_rows[pl.ds(k, NB, stride=FEAT), :] = row
        for g in range(4):
            moments[pl.ds(part * NB + g * 16, 16)] = (
                moment_rows[g * 16 * FEAT : (g + 1) * 16 * FEAT, :].reshape(16, FEAT, PB).astype(BF16)
            )
        if source is own:
            rows = []
            for h, m, l in splits:
                rows += [-2.0 * h, -2.0 * m, -2.0 * l, -2.0 * h, -2.0 * m, -2.0 * h]
            floored = split3(
                centred[0] * centred[0] + centred[1] * centred[1] + centred[2] * centred[2] + FLOOR_SQ
            )
            rows += list(floored) + [one] * 3
            rows += [zero] * (FEAT - len(rows))
            reach_rows = [zero] * 18 + list(reach) + [zero] * 3 + [one] * 3
            reach_rows += [zero] * (FEAT - len(reach_rows))
            for half, half_rows in enumerate((rows, reach_rows)):
                for k, row in enumerate(half_rows):
                    feat_rows[pl.ds(k, NB, stride=FEAT), :] = row
                for g in range(4):
                    own_feat[pl.ds(g * 16, 16), :, half * PB : (half + 1) * PB] = (
                        feat_rows[g * 16 * FEAT : (g + 1) * 16 * FEAT, :].reshape(16, FEAT, PB).astype(BF16)
                    )

    copies[0].wait()

    def partners(i):
        return [NB + i] + [neighbours[k, i] for k in range(K)]

    def pair_scales(i, scales):
        weights = jnp.concatenate([own_feat[i]] * 4, axis=0)
        places = partners(i)
        for g in range(0, K + 1, GROUP):
            others = jnp.concatenate([feat[e >> 2] * lane_masks[e & 3] for e in places[g : g + GROUP]], axis=0)
            pair = jnp.dot(others, weights, preferred_element_type=F32)
            inverse = lax.rsqrt(pair[:, :PB])
            push = jnp.maximum(pair[:, PB:] * inverse - 1.0, 0.0)
            scales[g * PB : (g + GROUP) * PB, :PB] = push.astype(BF16)
            scales[g * PB : (g + GROUP) * PB, PB:] = (push * inverse).astype(BF16)

    def pair_sums(i, scales):
        basis = jnp.concatenate([moments[e] for e in partners(i)], axis=1)
        sums[i] = jnp.dot(basis, scales[...], preferred_element_type=F32)

    def blocks(j, carry):
        pair_scales(2 * j + 1, scales_odd)
        pair_sums(2 * j, scales_even)
        pair_scales(jnp.minimum(2 * j + 2, NB - 1), scales_even)
        pair_sums(2 * j + 1, scales_odd)
        return carry

    pair_scales(0, scales_even)
    lax.fori_loop(0, NB // 2, blocks, 0, unroll=4)

    for copy in copies[1:]:
        copy.wait()

    def summed(k, half):
        lanes = slice(half * PB, (half + 1) * PB)
        value = sums[:, k, lanes]
        if k:
            value = value + sums[:, k + 9, lanes] + sums[:, k + 18, lanes]
        return value

    centred = [own[a] - CENTRE for a in range(3)]
    weight = summed(0, 0)
    first = [summed(1 + a, 0) for a in range(3)]
    forces = [centred[a] * weight - first[a] for a in range(3)]
    mass = 8.0 * own[3] * own[3] * own[3]
    results = []
    for n, (a, b) in enumerate(PAIRS):
        results.append(
            (centred[a] * centred[b]) * weight - centred[a] * first[b] - centred[b] * first[a] + summed(4 + n, 0)
        )
    for f, value in enumerate(results + [own[3], cells[...].astype(F32)]):
        ready[pl.ds(f, NB, stride=TILE), :] = value

    moved = [velocity[a] + TIMESTEP * (forces[a] / mass + GRAVITY[a]) for a in range(3)]
    bent = summed(0, 1)
    fabric = [
        (centred[a] * centred[a]) * bent - 2.0 * (centred[a] * summed(1 + a, 1)) + summed(4 + a, 1)
        for a in range(3)
    ]
    state = [own[a] + TIMESTEP * moved[a] for a in range(3)] + moved + fabric[:2]
    for f, value in enumerate(state):
        rest[pl.ds(f, NB, stride=TILE), :] = value
    last[...] = fabric[2]

    clear_counts(counts)
    out[...] = jnp.zeros_like(out)
    out_rest[...] = jnp.zeros_like(out_rest)

    def place_block(i, carry):
        owner, rank = next_slot(owners, counts, i)
        here = pl.ds(pl.multiple_of(i * TILE, TILE), TILE)
        slot = pl.multiple_of((owner * CAP + rank) * TILE, TILE)
        out[pl.ds(slot, TILE), :] = ready[here, :]
        out_rest[pl.ds(pl.multiple_of(owner * REST + rank * TILE, TILE), TILE), :] = rest[here, :]
        out_rest[pl.ds(owner * REST + CAP * TILE + rank, 1), :] = last[pl.ds(i, 1), :]
        return carry

    lax.fori_loop(0, NB, place_block, 0, unroll=4)


def contact(even, neighbours, owners, near, own, far, velocity, cells):
    anywhere = pl.BlockSpec(memory_space=pl.ANY)
    return pl.pallas_call(
        contact_kernel,
        out_shape=(
            jax.ShapeDtypeStruct((BRICKS * CAP * TILE, PB), F32),
            jax.ShapeDtypeStruct((BRICKS * REST, PB), F32),
        ),
        in_specs=[smem(), anywhere, anywhere, vmem(), vmem(), vmem(), anywhere, anywhere],
        out_specs=(vmem(), vmem()),
        scratch_shapes=[
            pltpu.VMEM((4, PB, PB), BF16),
            pltpu.VMEM((NB * FEAT, PB), F32),
            pltpu.VMEM((3 * NB // 4, PB, PB), BF16),
            pltpu.VMEM((NB, FEAT, 2 * PB), BF16),
            pltpu.VMEM((NB * FEAT, PB), F32),
            pltpu.VMEM((3 * NB, FEAT, PB), BF16),
            pltpu.VMEM((NB, FEAT, 2 * PB), F32),
            pltpu.VMEM((NB * TILE, PB), F32),
            pltpu.VMEM((NB * TILE, PB), F32),
            pltpu.VMEM((NB, PB), F32),
            pltpu.SMEM((BRICKS,), jnp.int32),
            pltpu.SMEM((K, NB), jnp.int32),
            pltpu.SMEM((NB,), jnp.int32),
            pltpu.VMEM((3, NB, PB), F32),
            pltpu.VMEM((NB, PB), jnp.int32),
            pltpu.SemaphoreType.DMA((4,)),
            pltpu.VMEM(((K + 1) * PB, 2 * PB), BF16),
            pltpu.VMEM(((K + 1) * PB, 2 * PB), BF16),
        ],
        compiler_params=pltpu.CompilerParams(vmem_limit_bytes=62 * 1024 * 1024),
        cost_estimate=pl.CostEstimate(flops=20_000_000_000, bytes_accessed=8_000_000, transcendentals=9_437_184),
        name="contact",
    )(even, neighbours, owners, near, own, far, velocity, cells)


def tap(distance):
    weights = kernel_weights()
    value = jnp.zeros(distance.shape, F32)
    for t in range(RAD + 1):
        value = jnp.where(jnp.abs(distance) == t, weights[RAD + t], value)
    return value


def split2(value):
    high = value.astype(BF16)
    return high, (value - high.astype(F32)).astype(BF16)


def deposit_grid(grid, chunk_fields, early):
    grid[...] = jnp.zeros_like(grid)
    group = 8
    width = group * CAP * PB

    def chunk(c, carry):
        slots = [(c * group + s, q) for s in range(group) for q in range(CAP)]
        first = jnp.concatenate([early[s, TILE * q : TILE * (q + 1), :] for s, q in slots], axis=1)
        fields = chunk_fields(first, slots)
        cells = first[7:8].astype(jnp.int32)
        across = lax.broadcasted_iota(jnp.int32, (CZ * CY, width), 0) == cells // CX
        along = jnp.where(
            lax.broadcasted_iota(jnp.int32, (CX, width), 0) == cells % CX, 1.0, 0.0
        ).astype(BF16)
        weighted = jnp.concatenate(
            [jnp.where(across, field, 0.0).astype(BF16) for field in fields], axis=0
        )
        grid[...] += lax.dot_general(
            weighted, along, (((1,), (1,)), ((), ())), preferred_element_type=F32
        )
        return carry

    lax.fori_loop(0, BRICKS // group, chunk, 0)


def smooth_columns(slab_even, grid, tile, send_a, send_b):
    count = tile.shape[0]
    rows = lax.broadcasted_iota(jnp.int32, (CX, CX), 0)
    band_high, band_low = split2(tap(rows - lax.broadcasted_iota(jnp.int32, (CX, CX), 1)))

    def smooth(f, carry):
        high, low = split2(grid[pl.ds(pl.multiple_of(f * CZ * CY, CZ * CY), CZ * CY), :])
        value = jnp.dot(jnp.concatenate([high, low], axis=0), band_high, preferred_element_type=F32)
        tile[f] = value[: CZ * CY] + value[CZ * CY :] + jnp.dot(high, band_low, preferred_element_type=F32)
        return carry

    lax.fori_loop(0, count, smooth, 0, unroll=2)

    rows = RAD * CY
    top = CZ * CY - rows

    @pl.when(slab_even[0] == 1)
    def _():
        send_a[...] = tile[:, top:, :]
        send_b[...] = tile[:, :rows, :]

    @pl.when(slab_even[0] == 0)
    def _():
        send_a[...] = tile[:, :rows, :]
        send_b[...] = tile[:, top:, :]


def deposit_first_kernel(slab_even, early, tile, send_a, send_b, grid):
    deposit_grid(grid, lambda first, slots: [first[f : f + 1] for f in range(FIRST)], early)
    smooth_columns(slab_even, grid, tile, send_a, send_b)


def deposit_second_kernel(slab_even, early, late, tile, send_a, send_b, grid):
    def fields(first, slots):
        reach = first[6:7]
        fabric = jnp.concatenate([late[s, TILE * q + 6 : TILE * q + 8, :] for s, q in slots], axis=1)
        last = jnp.concatenate([late[s, CAP * TILE + q : CAP * TILE + q + 1, :] for s, q in slots], axis=1)
        return [8.0 * reach * reach * reach, fabric[:1], fabric[1:], last]

    deposit_grid(grid, fields, early)
    smooth_columns(slab_even, grid, tile, send_a, send_b)


def deposit(kernel, count, name, slab_even, *parts):
    side = jax.ShapeDtypeStruct((count, CZ * RAD, CX), F32)
    return pl.pallas_call(
        kernel,
        out_shape=(jax.ShapeDtypeStruct((count, CZ * CY, CX), F32), side, side),
        in_specs=[smem()] + [vmem()] * len(parts),
        out_specs=(vmem(), vmem(), vmem()),
        scratch_shapes=[pltpu.VMEM((count * CZ * CY, CX), F32)],
        compiler_params=pltpu.CompilerParams(vmem_limit_bytes=40 * 1024 * 1024),
        cost_estimate=pl.CostEstimate(flops=count * 1_200_000_000, bytes_accessed=4_000_000, transcendentals=0),
        name=name,
    )(slab_even, *parts)


def halo_weights(even, along_rows):
    def line(value):
        return value % CY if along_rows else value // CY

    def other(value):
        return value // CY if along_rows else value % CY

    def side_line(value):
        return value % RAD if along_rows else value // CY

    def side_other(value):
        return value // RAD if along_rows else value % CY

    def part(count, place, same):
        out = lax.broadcasted_iota(jnp.int32, (CZ * CY, count), 0)
        source = lax.broadcasted_iota(jnp.int32, (CZ * CY, count), 1)
        return jnp.where(other(out) == same(source), tap(place(source) - line(out)), 0.0)

    above = RAD * CY
    return jnp.concatenate(
        [
            part(CZ * CY, line, other),
            part(above, lambda v: side_line(v) + jnp.where(even == 1, CY, -RAD), side_other),
            part(above, lambda v: side_line(v) + jnp.where(even == 1, -RAD, CY), side_other),
        ],
        axis=1,
    )


def smooth_all(weights, tile, side_a, side_b, out, first=0):
    weight_high, weight_low = split2(weights)
    both = jnp.concatenate([weight_high, weight_low], axis=0)
    rows = CZ * CY

    def smooth(f, carry):
        value = jnp.concatenate([tile[f], side_a[f], side_b[f]], axis=0)
        high, low = split2(value)
        part = jnp.dot(both, high, preferred_element_type=F32)
        result = part[:rows] + part[rows:] + jnp.dot(weight_high, low, preferred_element_type=F32)
        out[first + f] = result.reshape(out.shape[1:])
        return carry

    lax.fori_loop(0, tile.shape[0], smooth, 0, unroll=2)


def smooth_layers_kernel(even, slab_even, tile, side_a, side_b, out, send_a, send_b):
    smooth_all(halo_weights(slab_even[0], False), tile, side_a, side_b, out)

    def border(target, first):
        for f in range(tile.shape[0]):
            for z in range(CZ):
                target[f, z * RAD : (z + 1) * RAD, :] = out[f, z * CY + first : z * CY + first + RAD, :]

    @pl.when(even[0] == 1)
    def _():
        border(send_a, CY - RAD)
        border(send_b, 0)

    @pl.when(even[0] == 0)
    def _():
        border(send_a, 0)
        border(send_b, CY - RAD)


def smooth_layers(even, slab_even, tile, side_a, side_b):
    count = tile.shape[0]
    side = jax.ShapeDtypeStruct((count, CZ * RAD, CX), F32)
    return pl.pallas_call(
        smooth_layers_kernel,
        out_shape=(jax.ShapeDtypeStruct((count, CZ * CY, CX), F32), side, side),
        in_specs=[smem(), smem(), vmem(), vmem(), vmem()],
        out_specs=(vmem(), vmem(), vmem()),
        compiler_params=pltpu.CompilerParams(vmem_limit_bytes=40 * 1024 * 1024),
        name="smooth_layers",
    )(even, slab_even, tile, side_a, side_b)


def smooth_rows_kernel(even, tile, side_a, side_b, tile2, side_a2, side_b2, out):
    weights = halo_weights(even[0], True)
    smooth_all(weights, tile, side_a, side_b, out)
    smooth_all(weights, tile2, side_a2, side_b2, out, FIRST)


def smooth_rows(even, *parts):
    return pl.pallas_call(
        smooth_rows_kernel,
        out_shape=jax.ShapeDtypeStruct((FIELDS, CZ, CY, CX), F32),
        in_specs=[smem()] + [vmem()] * len(parts),
        out_specs=vmem(),
        compiler_params=pltpu.CompilerParams(vmem_limit_bytes=40 * 1024 * 1024),
        name="smooth_rows",
    )(even, *parts)


def swap_near(value, axis, count):
    return lax.ppermute(value, axis, [(i, i ^ 1) for i in range(count)])


def swap_far(value, axis, count):
    return lax.ppermute(value, axis, [(i, i + 1 if i % 2 else i - 1) for i in range(1, count - 1)])


def to_owners(value):
    return lax.all_to_all(value.reshape(BRICKS, -1, PB), "brick", split_axis=0, concat_axis=0, tiled=True)


def swap_layers(even, slab_even, tile, send_a, send_b):
    side_a = swap_near(send_a, "slab", SLABS)
    side_b = swap_far(send_b, "slab", SLABS)
    return smooth_layers(even, slab_even, tile, side_a, side_b)


def swap_rows(layers, send_a, send_b):
    return layers, swap_near(send_a, "brick", BRICKS), swap_far(send_b, "brick", BRICKS)


def body(positions, velocities, radius, owners, neighbours, cell_index):
    even = (1 - (lax.axis_index("brick") & 1)).astype(jnp.int32).reshape(1)
    slab_even = (1 - (lax.axis_index("slab") & 1)).astype(jnp.int32).reshape(1)
    velocity = jnp.transpose(velocities, (1, 0, 2))
    packed = jnp.concatenate([jnp.transpose(positions, (1, 0, 2)), radius[None]], axis=0)
    near = swap_near(packed, "brick", BRICKS)
    far = swap_far(packed, "brick", BRICKS)
    first, rest = contact(even, neighbours.T, owners, near, packed, far, velocity, cell_index)
    first = to_owners(first)
    rest = to_owners(rest)
    tiles = deposit(deposit_first_kernel, FIRST, "deposit_first", slab_even, first)
    tiles2 = deposit(deposit_second_kernel, SECOND, "deposit_second", slab_even, first, rest)
    parts = swap_rows(*swap_layers(even, slab_even, *tiles))
    parts2 = swap_rows(*swap_layers(even, slab_even, *tiles2))
    arrived = rest[:, : CAP * TILE].reshape(BRICKS * CAP, TILE, PB)[:, :6]
    return arrived, smooth_rows(even, *parts, *parts2)


def solution(mesh):
    return jax.shard_map(
        body,
        mesh=mesh,
        in_specs=(
            P(("slab", "brick"), None, None),
            P(("slab", "brick"), None, None),
            P(("slab", "brick"), None),
            P(("slab", "brick")),
            P(("slab", "brick"), None),
            P(("slab", "brick"), None),
        ),
        out_specs=(P(("slab", "brick"), None, None), P(None, "slab", "brick", None)),
        check_vma=False,
    )
```

```python
import functools
import math

import jax
import jax.numpy as jnp
from jax import lax
from jax.experimental import pallas as pl
from jax.experimental.pallas import tpu as pltpu
from jax.sharding import PartitionSpec as P

FIELDS = 10
RAD = 3
CZ = 8
CY = 8
CX = 512
CAP = 4
NB = 64
PB = 128
K = 8
BRICKS = 32
SLABS = 8
TILE = 8
REST = 40
FIRST = 6
SECOND = 4
FEAT = 32
GROUP = 3

TIMESTEP = 0.1
FLOOR_SQ = 0.0625
GRAVITY = (0.5, 0.0, -0.866)
PAIRS = ((0, 0), (1, 1), (2, 2), (0, 1), (0, 2), (1, 2))
CENTRE = 4.5
BF16 = jnp.bfloat16
F32 = jnp.float32


def kernel_weights():
    raw = [math.exp(-(t * t) / 4.5) for t in range(-RAD, RAD + 1)]
    total = sum(raw)
    return [v / total for v in raw]


def split3(value):
    high = value.astype(BF16).astype(F32)
    rest = value - high
    mid = rest.astype(BF16).astype(F32)
    return high, mid, rest - mid


def vmem():
    return pl.BlockSpec(memory_space=pltpu.VMEM)


def smem():
    return pl.BlockSpec(memory_space=pltpu.SMEM)


def clear_counts(counts):
    def clear(o, carry):
        counts[o] = 0
        return carry

    lax.fori_loop(0, BRICKS, clear, 0)


def next_slot(owners, counts, i):
    owner = owners[i]
    rank = counts[owner]
    counts[owner] = rank + 1
    return owner, rank


def contact_kernel(
    even,
    neighbours_in,
    owners_in,
    near,
    own,
    far,
    velocity_in,
    cells_in,
    out,
    out_rest,
    lane_masks,
    feat,
    own_feat,
    moments,
    sums,
    ready,
    rest,
    last,
    counts,
    neighbours,
    owners,
    velocity,
    cells,
    copy_sems,
    scales_even,
    scales_odd,
):
    lane_group = lax.broadcasted_iota(jnp.int32, (PB, PB), 1) // FEAT
    for j in range(4):
        lane_masks[j] = jnp.where(lane_group == j, 1.0, 0.0).astype(BF16)
    copies = [
        pltpu.make_async_copy(source, target, copy_sems.at[n])
        for n, (source, target) in enumerate(
            ((neighbours_in, neighbours), (owners_in, owners), (velocity_in, velocity), (cells_in, cells))
        )
    ]
    for copy in copies:
        copy.start()
    near_part = 2 * even[0]
    for part, source in ((near_part, near), (1, own), (2 - near_part, far)):
        centred = [source[a] - CENTRE for a in range(3)]
        splits = [split3(c) for c in centred]
        norm = split3(centred[0] * centred[0] + centred[1] * centred[1] + centred[2] * centred[2])
        reach = split3(source[3])
        one = jnp.ones((NB, PB), F32)
        zero = jnp.zeros((NB, PB), F32)
        rows = []
        for h, m, l in splits:
            rows += [h, h, h, m, m, l]
        rows += [one] * 3 + list(norm) + list(reach)
        rows += [zero] * (FEAT - len(rows))
        spread = jnp.swapaxes(jnp.stack(rows), 0, 1)
        for g in range(NB // 4):
            feat[part * (NB // 4) + g] = spread[4 * g : 4 * g + 4].reshape(PB, PB).T.astype(BF16)
        x, y, z = centred
        basis = [x, y, z, x * x, y * y, z * z, x * y, x * z, y * z]
        parts = [split3(v) for v in basis]
        rows = [one] + [p[0] for p in parts] + [p[1] for p in parts] + [p[2] for p in parts]
        rows += [zero] * (FEAT - len(rows))
        moments[pl.ds(part * NB, NB)] = jnp.swapaxes(jnp.stack(rows), 0, 1).astype(BF16)
        if source is own:
            rows = []
            for h, m, l in splits:
                rows += [-2.0 * h, -2.0 * m, -2.0 * l, -2.0 * h, -2.0 * m, -2.0 * h]
            floored = split3(
                centred[0] * centred[0] + centred[1] * centred[1] + centred[2] * centred[2] + FLOOR_SQ
            )
            rows += list(floored) + [one] * 3
            rows += [zero] * (FEAT - len(rows))
            reach_rows = [zero] * 18 + list(reach) + [zero] * 3 + [one] * 3
            reach_rows += [zero] * (FEAT - len(reach_rows))
            for half, half_rows in enumerate((rows, reach_rows)):
                own_feat[:, :, half * PB : (half + 1) * PB] = jnp.swapaxes(jnp.stack(half_rows), 0, 1).astype(BF16)

    copies[0].wait()

    def partners(i):
        return [NB + i] + [neighbours[k, i] for k in range(K)]

    def pair_scales(i, scales):
        weights = jnp.concatenate([own_feat[i]] * 4, axis=0)
        places = partners(i)
        for g in range(0, K + 1, GROUP):
            others = jnp.concatenate([feat[e >> 2] * lane_masks[e & 3] for e in places[g : g + GROUP]], axis=0)
            pair = jnp.dot(others, weights, preferred_element_type=F32)
            inverse = lax.rsqrt(pair[:, :PB])
            push = jnp.maximum(pair[:, PB:] * inverse - 1.0, 0.0)
            scales[g * PB : (g + GROUP) * PB, :PB] = push.astype(BF16)
            scales[g * PB : (g + GROUP) * PB, PB:] = (push * inverse).astype(BF16)

    def pair_sums(i, scales):
        basis = jnp.concatenate([moments[e] for e in partners(i)], axis=1)
        sums[i] = jnp.dot(basis, scales[...], preferred_element_type=F32)

    def blocks(j, carry):
        pair_scales(2 * j + 1, scales_odd)
        pair_sums(2 * j, scales_even)
        pair_scales(jnp.minimum(2 * j + 2, NB - 1), scales_even)
        pair_sums(2 * j + 1, scales_odd)
        return carry

    pair_scales(0, scales_even)
    lax.fori_loop(0, NB // 2, blocks, 0, unroll=4)

    for copy in copies[1:]:
        copy.wait()

    def summed(k, half):
        lanes = slice(half * PB, (half + 1) * PB)
        value = sums[:, k, lanes]
        if k:
            value = value + sums[:, k + 9, lanes] + sums[:, k + 18, lanes]
        return value

    centred = [own[a] - CENTRE for a in range(3)]
    weight = summed(0, 0)
    first = [summed(1 + a, 0) for a in range(3)]
    forces = [centred[a] * weight - first[a] for a in range(3)]
    mass = 8.0 * own[3] * own[3] * own[3]
    results = []
    for n, (a, b) in enumerate(PAIRS):
        results.append(
            (centred[a] * centred[b]) * weight - centred[a] * first[b] - centred[b] * first[a] + summed(4 + n, 0)
        )
    for f, value in enumerate(results + [own[3], cells[...].astype(F32)]):
        ready[pl.ds(f, NB, stride=TILE), :] = value

    moved = [velocity[a] + TIMESTEP * (forces[a] / mass + GRAVITY[a]) for a in range(3)]
    bent = summed(0, 1)
    fabric = [
        (centred[a] * centred[a]) * bent - 2.0 * (centred[a] * summed(1 + a, 1)) + summed(4 + a, 1)
        for a in range(3)
    ]
    state = [own[a] + TIMESTEP * moved[a] for a in range(3)] + moved + fabric[:2]
    for f, value in enumerate(state):
        rest[pl.ds(f, NB, stride=TILE), :] = value
    last[...] = fabric[2]

    clear_counts(counts)
    out[...] = jnp.zeros_like(out)
    out_rest[...] = jnp.zeros_like(out_rest)

    def place_block(i, carry):
        owner, rank = next_slot(owners, counts, i)
        here = pl.ds(pl.multiple_of(i * TILE, TILE), TILE)
        slot = pl.multiple_of((owner * CAP + rank) * TILE, TILE)
        out[pl.ds(slot, TILE), :] = ready[here, :]
        out_rest[pl.ds(pl.multiple_of(owner * REST + rank * TILE, TILE), TILE), :] = rest[here, :]
        out_rest[pl.ds(owner * REST + CAP * TILE + rank, 1), :] = last[pl.ds(i, 1), :]
        return carry

    lax.fori_loop(0, NB, place_block, 0, unroll=4)


def contact(even, neighbours, owners, near, own, far, velocity, cells):
    anywhere = pl.BlockSpec(memory_space=pl.ANY)
    return pl.pallas_call(
        contact_kernel,
        out_shape=(
            jax.ShapeDtypeStruct((BRICKS * CAP * TILE, PB), F32),
            jax.ShapeDtypeStruct((BRICKS * REST, PB), F32),
        ),
        in_specs=[smem(), anywhere, anywhere, vmem(), vmem(), vmem(), anywhere, anywhere],
        out_specs=(vmem(), vmem()),
        scratch_shapes=[
            pltpu.VMEM((4, PB, PB), BF16),
            pltpu.VMEM((3 * NB // 4, PB, PB), BF16),
            pltpu.VMEM((NB, FEAT, 2 * PB), BF16),
            pltpu.VMEM((3 * NB, FEAT, PB), BF16),
            pltpu.VMEM((NB, FEAT, 2 * PB), F32),
            pltpu.VMEM((NB * TILE, PB), F32),
            pltpu.VMEM((NB * TILE, PB), F32),
            pltpu.VMEM((NB, PB), F32),
            pltpu.SMEM((BRICKS,), jnp.int32),
            pltpu.SMEM((K, NB), jnp.int32),
            pltpu.SMEM((NB,), jnp.int32),
            pltpu.VMEM((3, NB, PB), F32),
            pltpu.VMEM((NB, PB), jnp.int32),
            pltpu.SemaphoreType.DMA((4,)),
            pltpu.VMEM(((K + 1) * PB, 2 * PB), BF16),
            pltpu.VMEM(((K + 1) * PB, 2 * PB), BF16),
        ],
        compiler_params=pltpu.CompilerParams(vmem_limit_bytes=62 * 1024 * 1024),
        cost_estimate=pl.CostEstimate(flops=20_000_000_000, bytes_accessed=8_000_000, transcendentals=9_437_184),
        name="contact",
    )(even, neighbours, owners, near, own, far, velocity, cells)


def tap(distance):
    weights = kernel_weights()
    value = jnp.zeros(distance.shape, F32)
    for t in range(RAD + 1):
        value = jnp.where(jnp.abs(distance) == t, weights[RAD + t], value)
    return value


def split2(value):
    high = value.astype(BF16)
    return high, (value - high.astype(F32)).astype(BF16)


def deposit_grid(grid, chunk_fields, early):
    grid[...] = jnp.zeros_like(grid)
    group = 16
    width = group * CAP * PB

    def chunk(c, carry):
        slots = [(c * group + s, q) for s in range(group) for q in range(CAP)]
        first = jnp.concatenate([early[s, TILE * q : TILE * (q + 1), :] for s, q in slots], axis=1)
        fields = chunk_fields(first, slots)
        cells = first[7:8].astype(jnp.int32)
        across = lax.broadcasted_iota(jnp.int32, (CZ * CY, width), 0) == cells // CX
        along = jnp.where(
            lax.broadcasted_iota(jnp.int32, (CX, width), 0) == cells % CX, 1.0, 0.0
        ).astype(BF16)
        weighted = jnp.concatenate(
            [jnp.where(across, field, 0.0).astype(BF16) for field in fields], axis=0
        )
        grid[...] += lax.dot_general(
            weighted, along, (((1,), (1,)), ((), ())), preferred_element_type=F32
        )
        return carry

    lax.fori_loop(0, BRICKS // group, chunk, 0)


def smooth_columns(slab_even, grid, tile, send_a, send_b):
    count = tile.shape[0]
    rows = lax.broadcasted_iota(jnp.int32, (CX, CX), 0)
    band_high, band_low = split2(tap(rows - lax.broadcasted_iota(jnp.int32, (CX, CX), 1)))

    def smooth(f, carry):
        high, low = split2(grid[pl.ds(pl.multiple_of(f * CZ * CY, CZ * CY), CZ * CY), :])
        value = jnp.dot(jnp.concatenate([high, low], axis=0), band_high, preferred_element_type=F32)
        tile[f] = value[: CZ * CY] + value[CZ * CY :] + jnp.dot(high, band_low, preferred_element_type=F32)
        return carry

    lax.fori_loop(0, count, smooth, 0, unroll=2)

    rows = RAD * CY
    top = CZ * CY - rows

    @pl.when(slab_even[0] == 1)
    def _():
        send_a[...] = tile[:, top:, :]
        send_b[...] = tile[:, :rows, :]

    @pl.when(slab_even[0] == 0)
    def _():
        send_a[...] = tile[:, :rows, :]
        send_b[...] = tile[:, top:, :]


def deposit_first_kernel(slab_even, early, tile, send_a, send_b, grid):
    deposit_grid(grid, lambda first, slots: [first[f : f + 1] for f in range(FIRST)], early)
    smooth_columns(slab_even, grid, tile, send_a, send_b)


def deposit_second_kernel(slab_even, early, late, tile, send_a, send_b, grid):
    def fields(first, slots):
        reach = first[6:7]
        fabric = jnp.concatenate([late[s, TILE * q + 6 : TILE * q + 8, :] for s, q in slots], axis=1)
        last = jnp.concatenate([late[s, CAP * TILE + q : CAP * TILE + q + 1, :] for s, q in slots], axis=1)
        return [8.0 * reach * reach * reach, fabric[:1], fabric[1:], last]

    deposit_grid(grid, fields, early)
    smooth_columns(slab_even, grid, tile, send_a, send_b)


def deposit(kernel, count, name, slab_even, *parts):
    side = jax.ShapeDtypeStruct((count, CZ * RAD, CX), F32)
    return pl.pallas_call(
        kernel,
        out_shape=(jax.ShapeDtypeStruct((count, CZ * CY, CX), F32), side, side),
        in_specs=[smem()] + [vmem()] * len(parts),
        out_specs=(vmem(), vmem(), vmem()),
        scratch_shapes=[pltpu.VMEM((count * CZ * CY, CX), F32)],
        compiler_params=pltpu.CompilerParams(vmem_limit_bytes=40 * 1024 * 1024),
        cost_estimate=pl.CostEstimate(flops=count * 1_200_000_000, bytes_accessed=4_000_000, transcendentals=0),
        name=name,
    )(slab_even, *parts)


def halo_weights(even, along_rows):
    def line(value):
        return value % CY if along_rows else value // CY

    def other(value):
        return value // CY if along_rows else value % CY

    def side_line(value):
        return value % RAD if along_rows else value // CY

    def side_other(value):
        return value // RAD if along_rows else value % CY

    def part(count, place, same):
        out = lax.broadcasted_iota(jnp.int32, (CZ * CY, count), 0)
        source = lax.broadcasted_iota(jnp.int32, (CZ * CY, count), 1)
        return jnp.where(other(out) == same(source), tap(place(source) - line(out)), 0.0)

    above = RAD * CY
    return jnp.concatenate(
        [
            part(CZ * CY, line, other),
            part(above, lambda v: side_line(v) + jnp.where(even == 1, CY, -RAD), side_other),
            part(above, lambda v: side_line(v) + jnp.where(even == 1, -RAD, CY), side_other),
        ],
        axis=1,
    )


def smooth_all(weights, tile, side_a, side_b, out, first=0):
    weight_high, weight_low = split2(weights)
    both = jnp.concatenate([weight_high, weight_low], axis=0)
    rows = CZ * CY

    def smooth(f, carry):
        value = jnp.concatenate([tile[f], side_a[f], side_b[f]], axis=0)
        high, low = split2(value)
        part = jnp.dot(both, high, preferred_element_type=F32)
        result = part[:rows] + part[rows:] + jnp.dot(weight_high, low, preferred_element_type=F32)
        out[first + f] = result.reshape(out.shape[1:])
        return carry

    lax.fori_loop(0, tile.shape[0], smooth, 0, unroll=2)


def smooth_layers_kernel(even, slab_even, tile, side_a, side_b, out, send_a, send_b):
    smooth_all(halo_weights(slab_even[0], False), tile, side_a, side_b, out)

    def border(target, first):
        for f in range(tile.shape[0]):
            for z in range(CZ):
                target[f, z * RAD : (z + 1) * RAD, :] = out[f, z * CY + first : z * CY + first + RAD, :]

    @pl.when(even[0] == 1)
    def _():
        border(send_a, CY - RAD)
        border(send_b, 0)

    @pl.when(even[0] == 0)
    def _():
        border(send_a, 0)
        border(send_b, CY - RAD)


def smooth_layers(even, slab_even, tile, side_a, side_b):
    count = tile.shape[0]
    side = jax.ShapeDtypeStruct((count, CZ * RAD, CX), F32)
    return pl.pallas_call(
        smooth_layers_kernel,
        out_shape=(jax.ShapeDtypeStruct((count, CZ * CY, CX), F32), side, side),
        in_specs=[smem(), smem(), vmem(), vmem(), vmem()],
        out_specs=(vmem(), vmem(), vmem()),
        compiler_params=pltpu.CompilerParams(vmem_limit_bytes=40 * 1024 * 1024),
        name="smooth_layers",
    )(even, slab_even, tile, side_a, side_b)


def smooth_rows_kernel(first, even, tile, side_a, side_b, *rest):
    out, result, sem = rest[-3:]
    smooth_all(halo_weights(even[0], True), tile, side_a, side_b, result)
    copy = pltpu.make_async_copy(result, out.at[pl.ds(first, tile.shape[0])], sem)
    copy.start()
    copy.wait()


def smooth_rows(first, even, parts, into=None):
    anywhere = pl.BlockSpec(memory_space=pl.ANY)
    extra = () if into is None else (into,)
    return pl.pallas_call(
        functools.partial(smooth_rows_kernel, first),
        out_shape=jax.ShapeDtypeStruct((FIELDS, CZ, CY, CX), F32),
        in_specs=[smem()] + [vmem()] * 3 + [anywhere] * len(extra),
        out_specs=anywhere,
        scratch_shapes=[pltpu.VMEM((parts[0].shape[0], CZ, CY, CX), F32), pltpu.SemaphoreType.DMA],
        input_output_aliases={4: 0} if extra else {},
        compiler_params=pltpu.CompilerParams(vmem_limit_bytes=40 * 1024 * 1024),
        name="smooth_rows",
    )(even, *parts, *extra)


def swap_near(value, axis, count):
    return lax.ppermute(value, axis, [(i, i ^ 1) for i in range(count)])


def swap_far(value, axis, count):
    return lax.ppermute(value, axis, [(i, i + 1 if i % 2 else i - 1) for i in range(1, count - 1)])


def to_owners(value):
    return lax.all_to_all(value.reshape(BRICKS, -1, PB), "brick", split_axis=0, concat_axis=0, tiled=True)


def swap_layers(even, slab_even, tile, send_a, send_b):
    side_a = swap_near(send_a, "slab", SLABS)
    side_b = swap_far(send_b, "slab", SLABS)
    return smooth_layers(even, slab_even, tile, side_a, side_b)


def swap_rows(layers, send_a, send_b):
    return layers, swap_near(send_a, "brick", BRICKS), swap_far(send_b, "brick", BRICKS)


def body(positions, velocities, radius, owners, neighbours, cell_index):
    even = (1 - (lax.axis_index("brick") & 1)).astype(jnp.int32).reshape(1)
    slab_even = (1 - (lax.axis_index("slab") & 1)).astype(jnp.int32).reshape(1)
    velocity = jnp.transpose(velocities, (1, 0, 2))
    packed = jnp.concatenate([jnp.transpose(positions, (1, 0, 2)), radius[None]], axis=0)
    near = swap_near(packed, "brick", BRICKS)
    far = swap_far(packed, "brick", BRICKS)
    first, rest = contact(even, neighbours.T, owners, near, packed, far, velocity, cell_index)
    first = to_owners(first)
    rest = to_owners(rest)
    tiles = deposit(deposit_first_kernel, FIRST, "deposit_first", slab_even, first)
    tiles2 = deposit(deposit_second_kernel, SECOND, "deposit_second", slab_even, first, rest)
    parts = swap_rows(*swap_layers(even, slab_even, *tiles))
    parts2 = swap_rows(*swap_layers(even, slab_even, *tiles2))
    arrived = rest[:, : CAP * TILE].reshape(BRICKS * CAP, TILE, PB)[:, :6]
    field_grid = smooth_rows(0, even, parts)
    return arrived, smooth_rows(FIRST, even, parts2, field_grid)


def solution(mesh):
    return jax.shard_map(
        body,
        mesh=mesh,
        in_specs=(
            P(("slab", "brick"), None, None),
            P(("slab", "brick"), None, None),
            P(("slab", "brick"), None),
            P(("slab", "brick")),
            P(("slab", "brick"), None),
            P(("slab", "brick"), None),
        ),
        out_specs=(P(("slab", "brick"), None, None), P(None, "slab", "brick", None)),
        check_vma=False,
    )
```

```python
import functools
import math

import jax
import jax.numpy as jnp
from jax import lax
from jax.experimental import pallas as pl
from jax.experimental.pallas import tpu as pltpu
from jax.sharding import PartitionSpec as P

FIELDS = 10
RAD = 3
CZ = 8
CY = 8
CX = 512
CAP = 4
NB = 64
PB = 128
K = 8
BRICKS = 32
SLABS = 8
TILE = 8
REST = 9
FIRST = 6
SECOND = 4
FEAT = 32
GROUP = 3

TIMESTEP = 0.1
FLOOR_SQ = 0.0625
GRAVITY = (0.5, 0.0, -0.866)
PAIRS = ((0, 0), (1, 1), (2, 2), (0, 1), (0, 2), (1, 2))
CENTRE = 4.5
BF16 = jnp.bfloat16
F32 = jnp.float32


def kernel_weights():
    raw = [math.exp(-(t * t) / 4.5) for t in range(-RAD, RAD + 1)]
    total = sum(raw)
    return [v / total for v in raw]


def split3(value):
    high = value.astype(BF16).astype(F32)
    rest = value - high
    mid = rest.astype(BF16).astype(F32)
    return high, mid, rest - mid


def vmem():
    return pl.BlockSpec(memory_space=pltpu.VMEM)


def smem():
    return pl.BlockSpec(memory_space=pltpu.SMEM)


def clear_counts(counts):
    def clear(o, carry):
        counts[o] = 0
        return carry

    lax.fori_loop(0, BRICKS, clear, 0)


def next_slot(owners, counts, i):
    owner = owners[i]
    rank = counts[owner]
    counts[owner] = rank + 1
    return owner, rank


def contact_kernel(
    even,
    neighbours_in,
    owners_in,
    near,
    own,
    far,
    velocity_in,
    cells_in,
    out,
    out_rest,
    lane_masks,
    feat,
    own_feat,
    moments,
    sums,
    ready,
    rest,
    last,
    counts,
    neighbours,
    owners,
    velocity,
    cells,
    copy_sems,
    scales_even,
    scales_odd,
):
    lane_group = lax.broadcasted_iota(jnp.int32, (PB, PB), 1) // FEAT
    for j in range(4):
        lane_masks[j] = jnp.where(lane_group == j, 1.0, 0.0).astype(BF16)
    copies = [
        pltpu.make_async_copy(source, target, copy_sems.at[n])
        for n, (source, target) in enumerate(
            ((neighbours_in, neighbours), (owners_in, owners), (velocity_in, velocity), (cells_in, cells))
        )
    ]
    for copy in copies:
        copy.start()
    near_part = 2 * even[0]
    for part, source in ((near_part, near), (1, own), (2 - near_part, far)):
        centred = [source[a] - CENTRE for a in range(3)]
        splits = [split3(c) for c in centred]
        norm = split3(centred[0] * centred[0] + centred[1] * centred[1] + centred[2] * centred[2])
        reach = split3(source[3])
        one = jnp.ones((NB, PB), F32)
        zero = jnp.zeros((NB, PB), F32)
        rows = []
        for h, m, l in splits:
            rows += [h, h, h, m, m, l]
        rows += [one] * 3 + list(norm) + list(reach)
        rows += [zero] * (FEAT - len(rows))
        spread = jnp.swapaxes(jnp.stack(rows), 0, 1)
        for g in range(NB // 4):
            feat[part * (NB // 4) + g] = spread[4 * g : 4 * g + 4].reshape(PB, PB).T.astype(BF16)
        x, y, z = centred
        basis = [x, y, z, x * x, y * y, z * z, x * y, x * z, y * z]
        parts = [split3(v) for v in basis]
        rows = [one] + [p[0] for p in parts] + [p[1] for p in parts] + [p[2] for p in parts]
        rows += [zero] * (FEAT - len(rows))
        moments[pl.ds(part * NB, NB)] = jnp.swapaxes(jnp.stack(rows), 0, 1).astype(BF16)
        if source is own:
            rows = []
            for h, m, l in splits:
                rows += [-2.0 * h, -2.0 * m, -2.0 * l, -2.0 * h, -2.0 * m, -2.0 * h]
            floored = split3(
                centred[0] * centred[0] + centred[1] * centred[1] + centred[2] * centred[2] + FLOOR_SQ
            )
            rows += list(floored) + [one] * 3
            rows += [zero] * (FEAT - len(rows))
            reach_rows = [zero] * 18 + list(reach) + [zero] * 3 + [one] * 3
            reach_rows += [zero] * (FEAT - len(reach_rows))
            for half, half_rows in enumerate((rows, reach_rows)):
                own_feat[:, :, half * PB : (half + 1) * PB] = jnp.swapaxes(jnp.stack(half_rows), 0, 1).astype(BF16)

    copies[0].wait()

    def partners(i):
        return [NB + i] + [neighbours[k, i] for k in range(K)]

    def pair_scales(i, scales):
        weights = jnp.concatenate([own_feat[i]] * 4, axis=0)
        places = partners(i)
        for g in range(0, K + 1, GROUP):
            others = jnp.concatenate([feat[e >> 2] * lane_masks[e & 3] for e in places[g : g + GROUP]], axis=0)
            pair = jnp.dot(others, weights, preferred_element_type=F32)
            inverse = lax.rsqrt(pair[:, :PB])
            push = jnp.maximum(pair[:, PB:] * inverse - 1.0, 0.0)
            scales[g * PB : (g + GROUP) * PB, :PB] = push.astype(BF16)
            scales[g * PB : (g + GROUP) * PB, PB:] = (push * inverse).astype(BF16)

    def pair_sums(i, scales):
        basis = jnp.concatenate([moments[e] for e in partners(i)], axis=1)
        sums[i] = jnp.dot(basis, scales[...], preferred_element_type=F32)

    def blocks(j, carry):
        pair_scales(2 * j + 1, scales_odd)
        pair_sums(2 * j, scales_even)
        pair_scales(jnp.minimum(2 * j + 2, NB - 1), scales_even)
        pair_sums(2 * j + 1, scales_odd)
        return carry

    pair_scales(0, scales_even)
    lax.fori_loop(0, NB // 2, blocks, 0, unroll=8)

    for copy in copies[1:]:
        copy.wait()

    def summed(k, half):
        lanes = slice(half * PB, (half + 1) * PB)
        value = sums[:, k, lanes]
        if k:
            value = value + sums[:, k + 9, lanes] + sums[:, k + 18, lanes]
        return value

    centred = [own[a] - CENTRE for a in range(3)]
    weight = summed(0, 0)
    first = [summed(1 + a, 0) for a in range(3)]
    forces = [centred[a] * weight - first[a] for a in range(3)]
    mass = 8.0 * own[3] * own[3] * own[3]
    results = []
    for n, (a, b) in enumerate(PAIRS):
        results.append(
            (centred[a] * centred[b]) * weight - centred[a] * first[b] - centred[b] * first[a] + summed(4 + n, 0)
        )
    for f, value in enumerate(results + [own[3], cells[...].astype(F32)]):
        ready[pl.ds(f, NB, stride=TILE), :] = value

    moved = [velocity[a] + TIMESTEP * (forces[a] / mass + GRAVITY[a]) for a in range(3)]
    bent = summed(0, 1)
    fabric = [
        (centred[a] * centred[a]) * bent - 2.0 * (centred[a] * summed(1 + a, 1)) + summed(4 + a, 1)
        for a in range(3)
    ]
    state = [own[a] + TIMESTEP * moved[a] for a in range(3)] + moved + fabric[:2]
    for f, value in enumerate(state):
        rest[pl.ds(f, NB, stride=TILE), :] = value
    last[...] = fabric[2]

    clear_counts(counts)
    out[...] = jnp.zeros_like(out)
    out_rest[...] = jnp.zeros_like(out_rest)

    def place_block(i, carry):
        owner, rank = next_slot(owners, counts, i)
        here = pl.ds(pl.multiple_of(i * TILE, TILE), TILE)
        slot = pl.multiple_of((owner * CAP + rank) * TILE, TILE)
        out[pl.ds(slot, TILE), :] = ready[here, :]
        for f in range(TILE):
            out_rest[owner, f, pl.ds(rank, 1), :] = rest[pl.ds(i * TILE + f, 1), :]
        out_rest[owner, TILE, pl.ds(rank, 1), :] = last[pl.ds(i, 1), :]
        return carry

    lax.fori_loop(0, NB, place_block, 0, unroll=4)


def contact(even, neighbours, owners, near, own, far, velocity, cells):
    anywhere = pl.BlockSpec(memory_space=pl.ANY)
    return pl.pallas_call(
        contact_kernel,
        out_shape=(
            jax.ShapeDtypeStruct((BRICKS * CAP * TILE, PB), F32),
            jax.ShapeDtypeStruct((BRICKS, REST, CAP, PB), F32),
        ),
        in_specs=[smem(), anywhere, anywhere, vmem(), vmem(), vmem(), anywhere, anywhere],
        out_specs=(vmem(), vmem()),
        scratch_shapes=[
            pltpu.VMEM((4, PB, PB), BF16),
            pltpu.VMEM((3 * NB // 4, PB, PB), BF16),
            pltpu.VMEM((NB, FEAT, 2 * PB), BF16),
            pltpu.VMEM((3 * NB, FEAT, PB), BF16),
            pltpu.VMEM((NB, FEAT, 2 * PB), F32),
            pltpu.VMEM((NB * TILE, PB), F32),
            pltpu.VMEM((NB * TILE, PB), F32),
            pltpu.VMEM((NB, PB), F32),
            pltpu.SMEM((BRICKS,), jnp.int32),
            pltpu.SMEM((K, NB), jnp.int32),
            pltpu.SMEM((NB,), jnp.int32),
            pltpu.VMEM((3, NB, PB), F32),
            pltpu.VMEM((NB, PB), jnp.int32),
            pltpu.SemaphoreType.DMA((4,)),
            pltpu.VMEM(((K + 1) * PB, 2 * PB), BF16),
            pltpu.VMEM(((K + 1) * PB, 2 * PB), BF16),
        ],
        compiler_params=pltpu.CompilerParams(vmem_limit_bytes=62 * 1024 * 1024),
        cost_estimate=pl.CostEstimate(flops=20_000_000_000, bytes_accessed=8_000_000, transcendentals=9_437_184),
        name="contact",
    )(even, neighbours, owners, near, own, far, velocity, cells)


def tap(distance):
    weights = kernel_weights()
    value = jnp.zeros(distance.shape, F32)
    for t in range(RAD + 1):
        value = jnp.where(jnp.abs(distance) == t, weights[RAD + t], value)
    return value


def split2(value):
    high = value.astype(BF16)
    return high, (value - high.astype(F32)).astype(BF16)


def deposit_grid(grid, chunk_fields, early):
    grid[...] = jnp.zeros_like(grid)
    group = 32
    width = group * CAP * PB

    def chunk(c, carry):
        slots = [(c * group + s, q) for s in range(group) for q in range(CAP)]
        first = jnp.concatenate([early[s, TILE * q : TILE * (q + 1), :] for s, q in slots], axis=1)
        fields = chunk_fields(first, slots)
        cells = first[7:8].astype(jnp.int32)
        across = lax.broadcasted_iota(jnp.int32, (CZ * CY, width), 0) == cells // CX
        along = jnp.where(
            lax.broadcasted_iota(jnp.int32, (CX, width), 0) == cells % CX, 1.0, 0.0
        ).astype(BF16)
        weighted = jnp.concatenate(
            [jnp.where(across, field, 0.0).astype(BF16) for field in fields], axis=0
        )
        grid[...] += lax.dot_general(
            weighted, along, (((1,), (1,)), ((), ())), preferred_element_type=F32
        )
        return carry

    lax.fori_loop(0, BRICKS // group, chunk, 0)


def smooth_columns(slab_even, grid, tile, send_a, send_b):
    count = tile.shape[0]
    rows = lax.broadcasted_iota(jnp.int32, (CX, CX), 0)
    band_high, band_low = split2(tap(rows - lax.broadcasted_iota(jnp.int32, (CX, CX), 1)))

    def smooth(f, carry):
        high, low = split2(grid[pl.ds(pl.multiple_of(f * CZ * CY, CZ * CY), CZ * CY), :])
        value = jnp.dot(jnp.concatenate([high, low], axis=0), band_high, preferred_element_type=F32)
        tile[f] = value[: CZ * CY] + value[CZ * CY :] + jnp.dot(high, band_low, preferred_element_type=F32)
        return carry

    lax.fori_loop(0, count, smooth, 0, unroll=2)

    rows = RAD * CY
    top = CZ * CY - rows

    @pl.when(slab_even[0] == 1)
    def _():
        send_a[...] = tile[:, top:, :]
        send_b[...] = tile[:, :rows, :]

    @pl.when(slab_even[0] == 0)
    def _():
        send_a[...] = tile[:, :rows, :]
        send_b[...] = tile[:, top:, :]


def deposit_first_kernel(slab_even, early, tile, send_a, send_b, grid):
    deposit_grid(grid, lambda first, slots: [first[f : f + 1] for f in range(FIRST)], early)
    smooth_columns(slab_even, grid, tile, send_a, send_b)


def deposit_second_kernel(slab_even, early, late, tile, send_a, send_b, grid):
    def fields(first, slots):
        reach = first[6:7]
        fabric = [jnp.concatenate([late[s, 6 + f, q : q + 1, :] for s, q in slots], axis=1) for f in range(3)]
        return [8.0 * reach * reach * reach] + fabric

    deposit_grid(grid, fields, early)
    smooth_columns(slab_even, grid, tile, send_a, send_b)


def deposit(kernel, count, name, slab_even, *parts):
    side = jax.ShapeDtypeStruct((count, CZ * RAD, CX), F32)
    return pl.pallas_call(
        kernel,
        out_shape=(jax.ShapeDtypeStruct((count, CZ * CY, CX), F32), side, side),
        in_specs=[smem()] + [vmem()] * len(parts),
        out_specs=(vmem(), vmem(), vmem()),
        scratch_shapes=[pltpu.VMEM((count * CZ * CY, CX), F32)],
        compiler_params=pltpu.CompilerParams(vmem_limit_bytes=40 * 1024 * 1024),
        cost_estimate=pl.CostEstimate(flops=count * 1_200_000_000, bytes_accessed=4_000_000, transcendentals=0),
        name=name,
    )(slab_even, *parts)


def halo_weights(even, along_rows):
    def line(value):
        return value % CY if along_rows else value // CY

    def other(value):
        return value // CY if along_rows else value % CY

    def side_line(value):
        return value % RAD if along_rows else value // CY

    def side_other(value):
        return value // RAD if along_rows else value % CY

    def part(count, place, same):
        out = lax.broadcasted_iota(jnp.int32, (CZ * CY, count), 0)
        source = lax.broadcasted_iota(jnp.int32, (CZ * CY, count), 1)
        return jnp.where(other(out) == same(source), tap(place(source) - line(out)), 0.0)

    above = RAD * CY
    return jnp.concatenate(
        [
            part(CZ * CY, line, other),
            part(above, lambda v: side_line(v) + jnp.where(even == 1, CY, -RAD), side_other),
            part(above, lambda v: side_line(v) + jnp.where(even == 1, -RAD, CY), side_other),
        ],
        axis=1,
    )


def smooth_all(weights, tile, side_a, side_b, out, first=0):
    weight_high, weight_low = split2(weights)
    both = jnp.concatenate([weight_high, weight_low], axis=0)
    rows = CZ * CY

    def smooth(f, carry):
        value = jnp.concatenate([tile[f], side_a[f], side_b[f]], axis=0)
        high, low = split2(value)
        part = jnp.dot(both, high, preferred_element_type=F32)
        result = part[:rows] + part[rows:] + jnp.dot(weight_high, low, preferred_element_type=F32)
        out[first + f] = result.reshape(out.shape[1:])
        return carry

    lax.fori_loop(0, tile.shape[0], smooth, 0, unroll=2)


def smooth_layers_kernel(even, slab_even, tile, side_a, side_b, out, send_a, send_b):
    smooth_all(halo_weights(slab_even[0], False), tile, side_a, side_b, out)

    def border(target, first):
        for f in range(tile.shape[0]):
            for z in range(CZ):
                target[f, z * RAD : (z + 1) * RAD, :] = out[f, z * CY + first : z * CY + first + RAD, :]

    @pl.when(even[0] == 1)
    def _():
        border(send_a, CY - RAD)
        border(send_b, 0)

    @pl.when(even[0] == 0)
    def _():
        border(send_a, 0)
        border(send_b, CY - RAD)


def smooth_layers(even, slab_even, tile, side_a, side_b):
    count = tile.shape[0]
    side = jax.ShapeDtypeStruct((count, CZ * RAD, CX), F32)
    return pl.pallas_call(
        smooth_layers_kernel,
        out_shape=(jax.ShapeDtypeStruct((count, CZ * CY, CX), F32), side, side),
        in_specs=[smem(), smem(), vmem(), vmem(), vmem()],
        out_specs=(vmem(), vmem(), vmem()),
        compiler_params=pltpu.CompilerParams(vmem_limit_bytes=40 * 1024 * 1024),
        name="smooth_layers",
    )(even, slab_even, tile, side_a, side_b)


def smooth_rows_kernel(first, even, tile, side_a, side_b, *rest):
    out, result, sem = rest[-3:]
    smooth_all(halo_weights(even[0], True), tile, side_a, side_b, result)
    copy = pltpu.make_async_copy(result, out.at[pl.ds(first, tile.shape[0])], sem)
    copy.start()
    copy.wait()


def smooth_rows(first, even, parts, into=None):
    anywhere = pl.BlockSpec(memory_space=pl.ANY)
    extra = () if into is None else (into,)
    return pl.pallas_call(
        functools.partial(smooth_rows_kernel, first),
        out_shape=jax.ShapeDtypeStruct((FIELDS, CZ, CY, CX), F32),
        in_specs=[smem()] + [vmem()] * 3 + [anywhere] * len(extra),
        out_specs=anywhere,
        scratch_shapes=[pltpu.VMEM((parts[0].shape[0], CZ, CY, CX), F32), pltpu.SemaphoreType.DMA],
        input_output_aliases={4: 0} if extra else {},
        compiler_params=pltpu.CompilerParams(vmem_limit_bytes=40 * 1024 * 1024),
        name="smooth_rows",
    )(even, *parts, *extra)


def swap_near(value, axis, count):
    return lax.ppermute(value, axis, [(i, i ^ 1) for i in range(count)])


def swap_far(value, axis, count):
    return lax.ppermute(value, axis, [(i, i + 1 if i % 2 else i - 1) for i in range(1, count - 1)])


def to_owners(value):
    return lax.all_to_all(value, "brick", split_axis=0, concat_axis=0, tiled=True)


def swap_layers(even, slab_even, tile, send_a, send_b):
    side_a = swap_near(send_a, "slab", SLABS)
    side_b = swap_far(send_b, "slab", SLABS)
    return smooth_layers(even, slab_even, tile, side_a, side_b)


def swap_rows(layers, send_a, send_b):
    return layers, swap_near(send_a, "brick", BRICKS), swap_far(send_b, "brick", BRICKS)


def body(positions, velocities, radius, owners, neighbours, cell_index):
    even = (1 - (lax.axis_index("brick") & 1)).astype(jnp.int32).reshape(1)
    slab_even = (1 - (lax.axis_index("slab") & 1)).astype(jnp.int32).reshape(1)
    velocity = jnp.transpose(velocities, (1, 0, 2))
    packed = jnp.concatenate([jnp.transpose(positions, (1, 0, 2)), radius[None]], axis=0)
    near = swap_near(packed, "brick", BRICKS)
    far = swap_far(packed, "brick", BRICKS)
    first, rest = contact(even, neighbours.T, owners, near, packed, far, velocity, cell_index)
    first = to_owners(first.reshape(BRICKS, CAP * TILE, PB))
    rest = to_owners(rest)
    tiles = deposit(deposit_first_kernel, FIRST, "deposit_first", slab_even, first)
    tiles2 = deposit(deposit_second_kernel, SECOND, "deposit_second", slab_even, first, rest)
    parts = swap_rows(*swap_layers(even, slab_even, *tiles))
    parts2 = swap_rows(*swap_layers(even, slab_even, *tiles2))
    arrived = jnp.transpose(rest[:, :6], (0, 2, 1, 3)).reshape(BRICKS * CAP, 6, PB)
    field_grid = smooth_rows(0, even, parts)
    return arrived, smooth_rows(FIRST, even, parts2, field_grid)


def solution(mesh):
    return jax.shard_map(
        body,
        mesh=mesh,
        in_specs=(
            P(("slab", "brick"), None, None),
            P(("slab", "brick"), None, None),
            P(("slab", "brick"), None),
            P(("slab", "brick")),
            P(("slab", "brick"), None),
            P(("slab", "brick"), None),
        ),
        out_specs=(P(("slab", "brick"), None, None), P(None, "slab", "brick", None)),
        check_vma=False,
    )
```
